128 devices in a mesh: lat: 16 (over y, z_lo, core), lon: 8 (over x, z_hi).
Axes of the slice: x: 4, y: 4, z: 4 (z_hi: 2, z_lo: 2; z = z_hi * 2 + z_lo), core: 2. Of those that a mesh axis runs over, the one named last changes fastest.
Arguments:
- patches: bfloat16 [4, 192, 96, 512], P(None, 'lat', 'lon'), may hold values from -6 to 6
- w_query: bfloat16 [512, 512], replicated, may hold values from -5 to 5
- w_keyval: bfloat16 [512, 1024], replicated, may hold values from -5 to 5
- w_out: bfloat16 [512, 512], replicated, may hold values from -0.25 to 0.25
- w_up: bfloat16 [512, 2048], replicated, may hold values from -0.25 to 0.25
- w_down: bfloat16 [2048, 512], replicated, may hold values from -0.125 to 0.125
- w_merge: bfloat16 [2048, 1024], replicated, may hold values from -0.125 to 0.125
- gain_attn: float32 [512], replicated, may hold values from 0.1 to 1.9
- gain_mlp: float32 [512], replicated, may hold values from 0.1 to 1.9
- gain_merge: float32 [2048], replicated, may hold values from 0.1 to 1.9
- lat_valid: int32 [192], replicated, may hold values 0 or 1
- region_ids: int32 [192], replicated, may hold values from 0 to 24, as said below
Outputs:
- merged: bfloat16 [4, 96, 48, 1024], P(None, 'lat', 'lon')
The draws below stay inside these ranges and needn't reach their ends.
Inputs may be any that keep to these rules, and one draw needn't show every extreme that they name: `region_ids`: region ids never fall along latitude, start at 0 and rise by one at exactly 24 rows; no rise lies at rows 91 to 102.
All inputs are finite; a program needn't handle non-finite values.
Results may differ from the reference program's by a relative error of at most 0.012.
Values may be sent and summed in bfloat16 or wider, within the bound.
A program may use at most 192 MiB of HBM per device.

```python
import jax
import jax.numpy as jnp
from jax import lax

D = 512
HEADS = 16
FFN = 2048
MERGED = 1024
LEVELS = 4
WIN_LEV = 2
WIN_LAT = 12
WIN_LON = 6
SHIFT_LEV = 1
SHIFT_LAT = 6
SHIFT_LON = 3
LAT = 192
LON = 96


def shared_base(key):
    return jnp.clip(jax.random.normal(key, (D, D), jnp.float32), -4.0, 4.0)


def draw_w_query(key, part):
    base_matrix = shared_base(key)
    values = base_matrix * D ** (-0.5)
    return values.astype(jnp.bfloat16)


def draw_w_keyval(key, part):
    key = jax.random.fold_in(key, 12)
    first_key, second_key = jax.random.split(key)
    noise = jnp.clip(jax.random.normal(first_key, (D, D), jnp.float32), -4.0, 4.0)
    value_part = jnp.clip(jax.random.normal(second_key, (D, D), jnp.float32), -4.0, 4.0) * D ** (-0.5)
    key_part = noise * D ** (-0.5)
    return jnp.concatenate([key_part, value_part], axis=1).astype(jnp.bfloat16)


def draw_region_ids(key, part):
    key = jax.random.fold_in(key, 13)
    quiet_rows = 2 * SHIFT_LAT
    order = (jax.random.permutation(key, LAT - 1 - quiet_rows) + 1).astype(jnp.int32)
    rows_picked = jnp.where(order >= LAT // 2 - SHIFT_LAT + 1, order + quiet_rows, order).astype(jnp.int32)
    chosen = rows_picked[:LAT // 8]
    breaks = jnp.zeros((LAT,), jnp.int32).at[chosen].set(1)
    return jnp.cumsum(breaks).astype(jnp.int32)


def touch_ends(drawn, key, low, high):
    longest = drawn.shape.index(max(drawn.shape))
    spots = []
    for shift in (0, 1):
        where = [jax.random.randint(jax.random.fold_in(key, axis), (), 0, length) for axis, length in enumerate(drawn.shape)]
        where[longest] = (where[longest] + shift) % drawn.shape[longest]
        spots.append(tuple(where))
    return drawn.at[spots[0]].set(low).at[spots[1]].set(high)


def block_scale(stream_key, extent, shards, low, high):
    loudness, own = 1.0, jax.random.fold_in(stream_key, 6)
    for axis_at, blocks in shards:
        steps = jnp.exp(jax.random.uniform(jax.random.fold_in(own, axis_at), (blocks,), jnp.float32, low / len(shards), high / len(shards)))
        loudness = loudness * jnp.repeat(steps, extent[axis_at] // blocks).reshape([-1 if axis == axis_at else 1 for axis in range(len(extent))])
    return loudness


def centred(stream_key, dims, width, most, shards=(), dtype=jnp.bfloat16):
    array = width * jax.random.normal(stream_key, dims, jnp.float32)
    if shards:
        array = array * block_scale(stream_key, dims, shards, -0.22, 0.18)
    return jnp.clip(array, -most, most).astype(dtype)


def setup_inputs(seed: int = 0) -> dict:
    keys = jax.random.split(jax.random.key(seed), 13)
    patches = centred(keys[0], (LEVELS, LAT, LON, D), 1.0, 6.0, ((1, 16), (2, 8)))
    w_query = draw_w_query(jax.random.fold_in(keys[12], 71), 0)
    w_keyval = draw_w_keyval(jax.random.fold_in(keys[12], 71), 0)
    w_out = centred(keys[3], (D, D), D ** -0.5, 0.25)
    w_up = centred(keys[4], (D, FFN), D ** -0.5, 0.25)
    w_down = centred(keys[5], (FFN, D), FFN ** -0.5, 0.125)
    w_merge = centred(keys[6], (4 * D, MERGED), (4 * D) ** -0.5, 0.125)
    gain_attn = jnp.clip(1.0 + 0.18 * jax.random.normal(keys[7], (D,), jnp.float32), 0.1, 1.9)
    gain_mlp = jnp.clip(1.0 + 0.18 * jax.random.normal(keys[8], (D,), jnp.float32), 0.1, 1.9)
    gain_merge = jnp.clip(1.0 + 0.18 * jax.random.normal(keys[9], (4 * D,), jnp.float32), 0.1, 1.9)
    lat_valid = touch_ends((jax.random.randint(keys[10], (LAT,), 0, 16) < 15).astype(jnp.int32), jax.random.fold_in(keys[10], 1), 0, 1)
    region_ids = draw_region_ids(jax.random.fold_in(keys[12], 71), 0)
    return dict(patches=patches, w_query=w_query, w_keyval=w_keyval, w_out=w_out, w_up=w_up, w_down=w_down, w_merge=w_merge, gain_attn=gain_attn, gain_mlp=gain_mlp, gain_merge=gain_merge, lat_valid=lat_valid, region_ids=region_ids)


EPSILON = 1e-05

def layer_norm(values, gain_vector):
    wide = values.astype(jnp.float32)
    average = lax.optimization_barrier(jnp.mean(wide, axis=-1, keepdims=True))
    variance = lax.optimization_barrier(jnp.mean((wide - average) ** 2, axis=-1, keepdims=True))
    return (wide - average) * lax.rsqrt(variance + EPSILON) * gain_vector.astype(jnp.float32)

def level_regions(level_count):
    levels = jnp.arange(level_count)
    return jnp.where(levels < SHIFT_LEV, 2, jnp.where(levels >= level_count - SHIFT_LEV, 1, 0)).astype(jnp.int32)

def to_windows(values_grid):
    level_count, row_count, col_count = values_grid.shape[:3]
    trailing = values_grid.shape[3:]
    shaped = values_grid.reshape((level_count // WIN_LEV, WIN_LEV, row_count // WIN_LAT, WIN_LAT, col_count // WIN_LON, WIN_LON) + trailing)
    order = (0, 2, 4, 1, 3, 5) + tuple(range(6, 6 + len(trailing)))
    return shaped.transpose(order).reshape((level_count // WIN_LEV, -1, WIN_LEV * WIN_LAT * WIN_LON) + trailing)

def from_windows(windows, level_count, row_count, col_count):
    trailing = windows.shape[3:]
    shaped = windows.reshape((level_count // WIN_LEV, row_count // WIN_LAT, col_count // WIN_LON, WIN_LEV, WIN_LAT, WIN_LON) + trailing)
    order = (0, 3, 1, 4, 2, 5) + tuple(range(6, 6 + len(trailing)))
    return shaped.transpose(order).reshape((level_count, row_count, col_count) + trailing)

def window_attention(inputs):
    queries, key_value, region_keys, valid_keys = inputs
    window_count, window_size, feature_width = queries.shape
    head_width = feature_width // HEADS
    q_heads = queries.astype(jnp.float32).reshape(window_count, window_size, HEADS, head_width)
    k_heads = key_value[..., :feature_width].astype(jnp.float32).reshape(window_count, window_size, HEADS, head_width)
    v_heads = key_value[..., feature_width:].astype(jnp.float32).reshape(window_count, window_size, HEADS, head_width)
    scores = jnp.einsum('wqhe,wkhe->whqk', q_heads, k_heads) * head_width ** (-0.5)
    same_region = region_keys[:, :, None] == region_keys[:, None, :]
    self_pair = jnp.arange(window_size)[:, None] == jnp.arange(window_size)[None, :]
    allowed = same_region & ((valid_keys[:, None, :] == 1) | self_pair[None])
    scores = jnp.where(allowed[:, None], scores, -jnp.inf)
    row_max = lax.optimization_barrier(jnp.max(scores, axis=-1, keepdims=True))
    probabilities = jnp.exp(scores - row_max)
    row_total = lax.optimization_barrier(jnp.sum(probabilities, axis=-1, keepdims=True))
    attn_weights = (probabilities / row_total).astype(jnp.bfloat16)
    attended = jnp.einsum('whqk,wkhe->wqhe', attn_weights.astype(jnp.float32), v_heads)
    return attended.astype(jnp.bfloat16).reshape(window_count, window_size, feature_width)

def grid_attention(queries, key_value, region_keys, valid_keys):
    level_count, row_count, col_count = queries.shape[:3]
    attended = lax.map(window_attention, (to_windows(queries), to_windows(key_value), to_windows(region_keys), to_windows(valid_keys)))
    return from_windows(attended, level_count, row_count, col_count)

def patch_merge(values_grid, gain_vector, weight):
    level_count, row_count, col_count, feature_width = values_grid.shape
    grouped = values_grid.reshape(level_count, row_count // 2, 2, col_count // 2, 2, feature_width)
    grouped = grouped.transpose(0, 1, 3, 4, 2, 5).reshape(level_count, row_count // 2, col_count // 2, 4 * feature_width)
    merge_normed = layer_norm(grouped, gain_vector).astype(jnp.bfloat16)
    return jnp.dot(merge_normed, weight, preferred_element_type=jnp.float32).astype(jnp.bfloat16)

def feed_forward(patches, attended, w_out, w_up, w_down, gain_mlp):
    after_attention = (patches.astype(jnp.float32) + jnp.dot(attended, w_out, preferred_element_type=jnp.float32)).astype(jnp.bfloat16)
    normed = layer_norm(after_attention, gain_mlp).astype(jnp.bfloat16)
    hidden = jax.nn.gelu(jnp.dot(normed, w_up, preferred_element_type=jnp.float32), approximate=False).astype(jnp.bfloat16)
    return (after_attention.astype(jnp.float32) + jnp.dot(hidden, w_down, preferred_element_type=jnp.float32)).astype(jnp.bfloat16)

def reference(patches, w_query, w_keyval, w_out, w_up, w_down, w_merge, gain_attn, gain_mlp, gain_merge, lat_valid, region_ids):
    level_count, row_count, col_count, feature_width = patches.shape
    normed = layer_norm(patches, gain_attn).astype(jnp.bfloat16)
    queries = jnp.dot(normed, w_query, preferred_element_type=jnp.float32).astype(jnp.bfloat16)
    key_value = jnp.dot(normed, w_keyval, preferred_element_type=jnp.float32).astype(jnp.bfloat16)
    shape3 = (level_count, row_count, col_count)
    region_keys = jnp.broadcast_to(region_ids[None, :, None] * 4 + level_regions(level_count)[:, None, None], shape3).astype(jnp.int32)
    valid_keys = jnp.broadcast_to(lat_valid[None, :, None], shape3).astype(jnp.int32)
    shifts = (-SHIFT_LEV, -SHIFT_LAT, -SHIFT_LON)
    rolled = [jnp.roll(item, shifts, axis=(0, 1, 2)) for item in (queries, key_value, region_keys, valid_keys)]
    band_count = row_count // WIN_LAT

    def banded(item):
        shaped = item.reshape((level_count, band_count, WIN_LAT) + item.shape[2:])
        return jnp.moveaxis(shaped, 1, 0)

    def band_attention(inputs):
        return grid_attention(inputs[0], inputs[1], inputs[2], inputs[3])
    bands = lax.map(band_attention, tuple((banded(item) for item in rolled)))
    attended = jnp.moveaxis(bands, 0, 1).reshape(level_count, row_count, col_count, feature_width)
    attended = jnp.roll(attended, (SHIFT_LEV, SHIFT_LAT, SHIFT_LON), axis=(0, 1, 2))
    after_mlp = feed_forward(patches, attended, w_out, w_up, w_down, gain_mlp)
    return patch_merge(after_mlp, gain_merge, w_merge)
```

```python
import functools
import math

import jax
import jax.numpy as jnp
import numpy as np
from jax import lax
from jax.experimental import pallas as pl
from jax.experimental.pallas import tpu as pltpu
from jax.sharding import PartitionSpec as P

HEADS = 16
D = 512
FFN = 2048
MERGED = 1024
WIN_LAT = 12
SHIFT_LAT = 6
EPSILON = 1e-05
MESH = pl.DeviceIdType.MESH
F32 = jnp.float32
BF16 = jnp.bfloat16

SEG_OWN, SEG_UP, SEG_LEFT, SEG_DIAG = (0, 112), (112, 112), (224, 48), (272, 48)
STAGE = 320
CELLS = 288
SLAB = 384
WINDOW = 144
LEVEL_PAIRS = ((1, 2), (3, 0))


def segment_of(lev, row, col):
    if row >= 6 and col >= 3:
        return (lev * 6 + row - 6) * 9 + col - 3
    if col >= 3:
        return 112 + (lev * 6 + row) * 9 + col - 3
    if row >= 6:
        return 224 + (lev * 6 + row - 6) * 3 + col
    return 272 + (lev * 6 + row) * 3 + col


def permutations():
    send = np.zeros((STAGE, SLAB), np.float32)
    to_win = np.zeros((CELLS, STAGE), np.float32)
    to_final = np.zeros((CELLS, STAGE), np.float32)
    slab_final = np.zeros((CELLS, SLAB), np.float32)
    for lev in range(2):
        for row in range(12):
            for col in range(12):
                slab = (lev * 12 + row) * 16 + col
                seg = segment_of(lev, row, col)
                send[seg, slab] = 1
                pos = (row % 2) + 2 * (col % 2)
                final = pos * 72 + lev * 36 + (row // 2) * 6 + col // 2
                to_final[final, seg] = 1
                slab_final[final, slab] = 1
                r, c = row + 6, col + 3
                source = segment_of(lev, r % 12, c % 12)
                group = col // 6
                win = group * WINDOW + lev * 72 + row * 6 + col - 6 * group
                to_win[win, source] = 1
    from_win = to_win.T.copy()
    out = np.zeros((192, 144), np.float32)
    for p, pair in enumerate(LEVEL_PAIRS):
        for slot, lev in enumerate(pair):
            for i in range(6):
                for j in range(6):
                    out[(lev * 6 + i) * 8 + j, p * 72 + slot * 36 + i * 6 + j] = 1
    return [m.astype(jnp.bfloat16) for m in (send, to_win, from_win, to_final, slab_final, out)]


def norm(wide, gain, width):
    average = jnp.sum(wide, axis=-1, keepdims=True) * (1.0 / width)
    centred = wide - average
    variance = jnp.sum(centred * centred, axis=-1, keepdims=True) * (1.0 / width)
    return centred * lax.rsqrt(variance + EPSILON) * gain


def dot(a, b):
    return jnp.dot(a, b, preferred_element_type=F32)


def kernel(
    lat_count,
    lon_count,
    x_hbm, wq_hbm, wkv_hbm, wo_hbm, wup_hbm, wdn_hbm, wm_hbm,
    send_hbm, towin_hbm, fromwin_hbm, tofinal_hbm, slabfinal_hbm, outperm_hbm,
    ga_ref, gm_ref, gg_ref, valid_ref, region_ref,
    out_ref,
    x_v, wq, wkv, wo, wup, wdn, wm,
    sendp, towin, fromwin, tofinal, slabfinal, outperm,
    slabs, sent, got, back, home, qkv, att, bias, resid, joined,
    local_sem, send_sem, recv_sem,
):
    a, o = lax.axis_index("lat"), lax.axis_index("lon")
    lat_dn = lax.rem(a + lat_count - 1, lat_count)
    lat_up = lax.rem(a + 1, lat_count)
    lon_dn = lax.rem(o + lon_count - 1, lon_count)
    lon_up = lax.rem(o + 1, lon_count)
    lower = ((lat_dn, o), (a, lon_dn), (lat_dn, lon_dn))
    upper = ((lat_up, o), (a, lon_up), (lat_up, lon_up))

    pairs = (
        (x_hbm, x_v), (send_hbm, sendp), (towin_hbm, towin), (wq_hbm, wq), (wkv_hbm, wkv),
        (slabfinal_hbm, slabfinal), (fromwin_hbm, fromwin), (tofinal_hbm, tofinal), (wo_hbm, wo),
        (wup_hbm, wup), (wdn_hbm, wdn), (wm_hbm, wm), (outperm_hbm, outperm),
    )
    loads = [pltpu.make_async_copy(s, d, local_sem.at[i]) for i, (s, d) in enumerate(pairs)]
    for load in loads:
        load.start()

    barrier = pltpu.get_barrier_semaphore()
    for device in lower + upper:
        pl.semaphore_signal(barrier, inc=1, device_id=device, device_id_type=MESH)

    slabs[...] = jnp.zeros_like(slabs)
    loads[0].wait()
    for p, pair in enumerate(LEVEL_PAIRS):
        for slot, lev in enumerate(pair):
            for row in range(12):
                slabs[p, slot * 12 + row, 0:12, :] = x_v[lev, row]

    loads[1].wait()
    pl.semaphore_wait(barrier, 6)

    def exchange(phase, p, source, target, devices):
        copies = []
        for i, (start, size) in enumerate((SEG_UP, SEG_LEFT, SEG_DIAG)):
            slot = (phase * 2 + p) * 3 + i
            copies.append(
                pltpu.make_async_remote_copy(
                    src_ref=source.at[p, pl.ds(start, size)],
                    dst_ref=target.at[p, pl.ds(start, size)],
                    send_sem=send_sem.at[slot],
                    recv_sem=recv_sem.at[slot],
                    device_id=devices[i],
                    device_id_type=MESH,
                )
            )
        for copy in copies:
            copy.start()
        return copies

    first = []
    for p in range(2):
        rows = slabs[p].reshape(SLAB, D)
        sent[p] = dot(sendp[...], rows).astype(BF16)
        first.append(exchange(0, p, sent, got, lower))

    key_row = lax.broadcasted_iota(jnp.int32, (WINDOW, 128), 0)
    key_lev = (key_row >= 72).astype(jnp.int32)
    key_lat = ((key_row - 72 * key_lev) * 683) >> 12
    start = a * WIN_LAT + SHIFT_LAT
    row_ids = [lax.rem(start + r, lat_count * WIN_LAT) for r in range(WIN_LAT)]
    tags = [region_ref[i] for i in row_ids]
    valid = [valid_ref[i] for i in row_ids]
    key_tag = jnp.zeros((WINDOW, 128), jnp.int32)
    key_valid = jnp.zeros((WINDOW, 128), jnp.int32)
    for r in range(WIN_LAT):
        key_tag = jnp.where(key_lat == r, tags[r], key_tag)
        key_valid = jnp.where(key_lat == r, valid[r], key_valid)
    lane = lax.broadcasted_iota(jnp.int32, (1, 128), 1) & 15
    for b in range(9):
        query = lane + 16 * b
        query_lev = (query >= 72).astype(jnp.int32)
        query_lat = ((query - 72 * query_lev) * 683) >> 12
        query_tag = jnp.zeros((1, 128), jnp.int32)
        for r in range(WIN_LAT):
            query_tag = jnp.where(query_lat == r, tags[r], query_tag)
        usable = (key_tag == query_tag) & ((key_valid == 1) | (key_row == query))
        bias[0, b] = jnp.where(usable, 0.0, -jnp.inf)
        bias[1, b] = jnp.where(usable & (key_lev == query_lev), 0.0, -jnp.inf)

    loads[5].wait()
    for p in range(2):
        resid[p] = dot(slabfinal[...], slabs[p].reshape(SLAB, D))

    for i in (2, 3, 4, 6):
        loads[i].wait()

    head_lane = lax.broadcasted_iota(jnp.int32, (16, 256), 1) >> 5
    head_mask = [(head_lane == h).astype(F32).astype(BF16) for h in range(8)]
    factor = math.log2(math.e) / math.sqrt(D // HEADS)

    second = []
    for p in range(2):
        for copy in first[p]:
            copy.wait_recv()
        staged = jnp.concatenate([sent[p, 0:112], got[p, 112:STAGE]], axis=0)
        cells = dot(towin[...], staged)
        normed = norm(cells, ga_ref[...], D).astype(BF16)
        qkv[:, 0:D] = dot(normed, wq[...]).astype(BF16)
        qkv[:, D : 3 * D] = dot(normed, wkv[...]).astype(BF16)

        def attend(step, carry):
            row0 = pl.multiple_of((step // 2) * WINDOW, 16)
            col0 = pl.multiple_of((step % 2) * 256, 256)
            keys = qkv[pl.ds(row0, WINDOW), pl.ds(pl.multiple_of(D + col0, 256), 256)]
            values = qkv[pl.ds(row0, WINDOW), pl.ds(pl.multiple_of(2 * D + col0, 256), 256)]
            for b in range(9):
                rows = pl.ds(pl.multiple_of(row0 + 16 * b, 16), 16)
                query = qkv[rows, pl.ds(col0, 256)]
                spread = jnp.concatenate([query * m for m in head_mask], axis=0)
                scores = lax.dot_general(
                    keys, spread, (((1,), (1,)), ((), ())), preferred_element_type=F32
                )
                scores = scores * factor + bias[p, b]
                top = jnp.max(scores, axis=0, keepdims=True)
                raised = jnp.exp2(scores - top)
                total = jnp.sum(raised, axis=0, keepdims=True)
                weights = (raised * (1.0 / total)).astype(BF16)
                wide = lax.dot_general(
                    weights, values, (((0,), (0,)), ((), ())), preferred_element_type=F32
                )
                mine = jnp.zeros((16, 256), F32)
                for h in range(8):
                    mine = jnp.where(head_lane == h, wide[16 * h : 16 * h + 16], mine)
                att[rows, pl.ds(col0, 256)] = mine.astype(BF16)
            return carry

        lax.fori_loop(0, 4, attend, 0)
        back[p] = dot(fromwin[...], att[...]).astype(BF16)
        second.append(exchange(1, p, back, home, upper))

    for i in (7, 8, 9, 10):
        loads[i].wait()
    for p in range(2):
        for copy in second[p]:
            copy.wait_recv()
        staged = jnp.concatenate([back[p, 0:112], home[p, 112:STAGE]], axis=0)
        attended = dot(tofinal[...], staged).astype(BF16)
        after = (resid[p] + dot(attended, wo[...])).astype(BF16)
        after_wide = after.astype(F32)
        normed = norm(after_wide, gm_ref[...], D).astype(BF16)
        total = after_wide
        for c in range(4):
            cols = slice(c * 512, c * 512 + 512)
            up = dot(normed, wup[:, cols])
            hidden = (0.5 * up * (1.0 + lax.erf(up * (2.0 ** -0.5)))).astype(BF16)
            total = total + dot(hidden, wdn[cols, :])
        done = total.astype(BF16).astype(F32)
        grouped = jnp.concatenate([done[72 * k : 72 * k + 72] for k in range(4)], axis=1)
        joined[72 * p : 72 * p + 72, :] = norm(grouped, gg_ref[...], 4 * D)

    loads[11].wait()
    loads[12].wait()
    merged = dot(joined[...].astype(BF16), wm[...]).astype(BF16)
    spaced = dot(outperm[...], merged).astype(BF16)
    for lev in range(4):
        for i in range(6):
            at = (lev * 6 + i) * 8
            out_ref[lev, i] = spaced[at : at + 8][0:6]
    for copy in first[0] + first[1] + second[0] + second[1]:
        copy.wait_send()


def on_device(
    lat_count, lon_count, patches, w_query, w_keyval, w_out, w_up, w_down, w_merge,
    gain_attn, gain_mlp, gain_merge, lat_valid, region_ids,
):
    perms = [jnp.asarray(m) for m in permutations()]
    hbm = pl.BlockSpec(memory_space=pl.ANY)
    vmem = pl.BlockSpec(memory_space=pltpu.VMEM)
    smem = pl.BlockSpec(memory_space=pltpu.SMEM)
    weights = (w_query, w_keyval, w_out, w_up, w_down, w_merge)
    held = [pltpu.VMEM(v.shape, v.dtype) for v in (patches,) + weights + tuple(perms)]
    return pl.pallas_call(
        functools.partial(kernel, lat_count, lon_count),
        out_shape=jax.ShapeDtypeStruct((4, 6, 6, MERGED), BF16),
        in_specs=[hbm] * 13 + [vmem] * 3 + [smem] * 2,
        out_specs=vmem,
        scratch_shapes=held
        + [
            pltpu.VMEM((2, 24, 16, D), BF16),
            pltpu.VMEM((2, STAGE, D), BF16),
            pltpu.VMEM((2, STAGE, D), BF16),
            pltpu.VMEM((2, STAGE, D), BF16),
            pltpu.VMEM((2, STAGE, D), BF16),
            pltpu.VMEM((CELLS, 3 * D), BF16),
            pltpu.VMEM((CELLS, D), BF16),
            pltpu.VMEM((2, 9, WINDOW, 128), F32),
            pltpu.VMEM((2, CELLS, D), F32),
            pltpu.VMEM((144, 4 * D), F32),
            pltpu.SemaphoreType.DMA((13,)),
            pltpu.SemaphoreType.DMA((12,)),
            pltpu.SemaphoreType.DMA((12,)),
        ],
        compiler_params=pltpu.CompilerParams(
            collective_id=0, has_side_effects=True, vmem_limit_bytes=56 * 1024 * 1024
        ),
        cost_estimate=pl.CostEstimate(
            flops=6_000_000_000, bytes_accessed=12_000_000, transcendentals=3_000_000
        ),
    )(
        patches, *weights, *perms,
        gain_attn.reshape(1, -1), gain_mlp.reshape(1, -1), gain_merge.reshape(1, -1),
        lat_valid, region_ids,
    )


def solution(mesh):
    placed = (P(None, "lat", "lon", None),) + (P(),) * 11
    return jax.shard_map(
        functools.partial(on_device, mesh.shape["lat"], mesh.shape["lon"]),
        mesh=mesh,
        in_specs=placed,
        out_specs=P(None, "lat", "lon", None),
        check_vma=False,
    )
```

```python
import functools
import math

import jax
import jax.numpy as jnp
import numpy as np
from jax import lax
from jax.experimental import pallas as pl
from jax.experimental.pallas import tpu as pltpu
from jax.sharding import PartitionSpec as P

HEADS = 16
D = 512
FFN = 2048
MERGED = 1024
WIN_LAT = 12
SHIFT_LAT = 6
EPSILON = 1e-05
MESH = pl.DeviceIdType.MESH
F32 = jnp.float32
BF16 = jnp.bfloat16

CELLS = 288
WINDOW = 144
LEVEL_SLOTS = (1, 2, 3, 0)
BACK_ROWS = (288, 320)
SEGMENTS = (((144, 144),), ((80, 80), (160, 80), (240, 80)))
MERGE_COLS = (((2, 3, 4), (1, 2, 3)), ((5, 0, 1), (4, 5, 0)))


def permutations():
    result = []
    for g in range(2):
        from_win = np.zeros((BACK_ROWS[g], CELLS), np.float32)
        to_final = np.zeros((CELLS, BACK_ROWS[g]), np.float32)
        flat_final = np.zeros((CELLS, 576), np.float32)
        for slot, lev in enumerate(LEVEL_SLOTS):
            for wr in range(12):
                for wc in range(6):
                    win = slot * 72 + wr * 6 + wc
                    if g == 0:
                        seg = (wr // 6) * 144 + slot * 36 + (wr % 6) * 6 + wc
                    else:
                        seg = (wr // 6 + 2 * (wc // 3)) * 80 + slot * 18 + (wr % 6) * 3 + wc % 3
                    row, col = (wr + 6) % 12, (wc + 3 + 6 * g) % 12
                    pos = row % 2 + 2 * (col % 2)
                    jslot = MERGE_COLS[g][col % 2].index(col // 2)
                    final = pos * 72 + jslot * 24 + (row // 2) * 4 + lev
                    from_win[seg, win] = 1
                    to_final[final, seg] = 1
                    flat_final[final, (row * 12 + col) * 4 + lev] = 1
        result += [from_win, to_final, flat_final]
    return [m.astype(jnp.bfloat16) for m in result]


def norm(wide, gain, width):
    average = jnp.sum(wide, axis=-1, keepdims=True) * (1.0 / width)
    centred = wide - average
    variance = jnp.sum(centred * centred, axis=-1, keepdims=True) * (1.0 / width)
    return centred * lax.rsqrt(variance + EPSILON) * gain


def dot(a, b):
    return jnp.dot(a, b, preferred_element_type=F32)


def kernel(
    lat_count,
    lon_count,
    x_hbm, wq_hbm, wkv_hbm, wo_hbm, wup_hbm, wdn_hbm, wm_hbm,
    fromwin0_hbm, tofinal0_hbm, flat0_hbm, fromwin1_hbm, tofinal1_hbm, flat1_hbm,
    ga_ref, gm_ref, gg_ref, valid_ref, region_ref,
    out_ref,
    x_v, wq, wkv, wo, wup, wdn, wm,
    fromwin0, tofinal0, flat0, fromwin1, tofinal1, flat1,
    cells0, cells1, back0, back1, home0, home1, wide, qkv, att, bias, resid, joined,
    local_sem, send_sem, recv_sem,
):
    a, o = lax.axis_index("lat"), lax.axis_index("lon")
    lat_dn = lax.rem(a + lat_count - 1, lat_count)
    lat_up = lax.rem(a + 1, lat_count)
    lon_dn = lax.rem(o + lon_count - 1, lon_count)
    lon_up = lax.rem(o + 1, lon_count)
    lower = ((lat_dn, o), (a, lon_dn), (lat_dn, lon_dn))
    upper = ((lat_up, o), (a, lon_up), (lat_up, lon_up))
    cells, back, home = (cells0, cells1), (back0, back1), (home0, home1)
    fromwin, tofinal, flat = (fromwin0, fromwin1), (tofinal0, tofinal1), (flat0, flat1)

    barrier = pltpu.get_barrier_semaphore()
    for device in lower + upper:
        pl.semaphore_signal(barrier, inc=1, device_id=device, device_id_type=MESH)

    pairs = (
        (x_hbm.at[pl.ds(6, 6), pl.ds(3, 6)], cells0.at[pl.ds(0, 6)]),
        (x_hbm.at[pl.ds(6, 6), pl.ds(9, 3)], cells1.at[pl.ds(0, 6), pl.ds(0, 3)]),
        (x_hbm, x_v), (wq_hbm, wq), (wkv_hbm, wkv), (flat0_hbm, flat0), (flat1_hbm, flat1),
        (fromwin0_hbm, fromwin0), (fromwin1_hbm, fromwin1),
        (tofinal0_hbm, tofinal0), (tofinal1_hbm, tofinal1),
        (wo_hbm, wo), (wup_hbm, wup), (wdn_hbm, wdn), (wm_hbm, wm),
    )
    loads = [pltpu.make_async_copy(s, d, local_sem.at[i]) for i, (s, d) in enumerate(pairs)]

    def remote(slot, source, target, device):
        return pltpu.make_async_remote_copy(
            src_ref=source, dst_ref=target, send_sem=send_sem.at[slot], recv_sem=recv_sem.at[slot],
            device_id=device, device_id_type=MESH,
        )

    first = [
        remote(0, x_hbm.at[pl.ds(0, 6), pl.ds(3, 6)], cells0.at[pl.ds(6, 6)], lower[0]),
        remote(1, x_hbm.at[pl.ds(0, 6), pl.ds(0, 3)], cells1.at[pl.ds(6, 6), pl.ds(3, 3)], lower[2]),
        remote(2, x_hbm.at[pl.ds(6, 6), pl.ds(0, 3)], cells1.at[pl.ds(0, 6), pl.ds(3, 3)], lower[1]),
        remote(3, x_hbm.at[pl.ds(0, 6), pl.ds(9, 3)], cells1.at[pl.ds(6, 6), pl.ds(0, 3)], lower[0]),
    ]
    for load in loads[:3]:
        load.start()
    pl.semaphore_wait(barrier, 6)
    for copy in first:
        copy.start()
    for load in loads[3:]:
        load.start()

    key_row = lax.broadcasted_iota(jnp.int32, (WINDOW, 128), 0)
    key_lev = (key_row >= 72).astype(jnp.int32)
    key_lat = ((key_row - 72 * key_lev) * 683) >> 12
    start = a * WIN_LAT + SHIFT_LAT
    row_ids = [lax.rem(start + r, lat_count * WIN_LAT) for r in range(WIN_LAT)]
    tags = [region_ref[i] for i in row_ids]
    valid = [valid_ref[i] for i in row_ids]
    key_tag = jnp.zeros((WINDOW, 128), jnp.int32)
    key_valid = jnp.zeros((WINDOW, 128), jnp.int32)
    for r in range(WIN_LAT):
        key_tag = jnp.where(key_lat == r, tags[r], key_tag)
        key_valid = jnp.where(key_lat == r, valid[r], key_valid)
    lane = lax.broadcasted_iota(jnp.int32, (1, 128), 1) & 15
    for b in range(9):
        query = lane + 16 * b
        query_lev = (query >= 72).astype(jnp.int32)
        query_lat = ((query - 72 * query_lev) * 683) >> 12
        query_tag = jnp.zeros((1, 128), jnp.int32)
        for r in range(WIN_LAT):
            query_tag = jnp.where(query_lat == r, tags[r], query_tag)
        usable = (key_tag == query_tag) & ((key_valid == 1) | (key_row == query))
        bias[0, b] = jnp.where(usable, 0.0, -jnp.inf)
        bias[1, b] = jnp.where(usable & (key_lev == query_lev), 0.0, -jnp.inf)

    for i in (2, 5, 6):
        loads[i].wait()
    mine = jnp.concatenate([x_v[r].astype(F32).reshape(48, D) for r in range(12)], axis=0).astype(BF16)
    for g in range(2):
        resid[g] = dot(flat[g][...], mine)

    head_lane = lax.broadcasted_iota(jnp.int32, (16, 256), 1) >> 5
    head_mask = [(head_lane == h).astype(F32).astype(BF16) for h in range(8)]
    factor = math.log2(math.e) / math.sqrt(D // HEADS)

    second = []
    for g in range(2):
        loads[g].wait()
        for copy in (first[:1], first[1:])[g]:
            copy.wait_recv()
        if g == 0:
            loads[3].wait()
            loads[4].wait()
        for row in range(12):
            flat_row = cells[g][row].astype(F32).reshape(24, D)
            for c in range(4):
                wide[c, 24 * row : 24 * row + 24, :] = flat_row[:, 128 * c : 128 * c + 128]
        levels = [
            jnp.concatenate([wide[c, pl.ds(lev, 72, stride=4), :] for c in range(4)], axis=1)
            for lev in LEVEL_SLOTS
        ]
        normed = norm(jnp.concatenate(levels, axis=0), ga_ref[...], D).astype(BF16)
        qkv[:, 0:D] = dot(normed, wq[...]).astype(BF16)
        qkv[:, D : 3 * D] = dot(normed, wkv[...]).astype(BF16)

        def attend(step, carry):
            window = step // 2
            row0 = pl.multiple_of(window * WINDOW, 16)
            col0 = pl.multiple_of((step % 2) * 256, 256)
            keys = qkv[pl.ds(row0, WINDOW), pl.ds(pl.multiple_of(D + col0, 256), 256)]
            values = qkv[pl.ds(row0, WINDOW), pl.ds(pl.multiple_of(2 * D + col0, 256), 256)]
            for b in range(9):
                rows = pl.ds(pl.multiple_of(row0 + 16 * b, 16), 16)
                query = qkv[rows, pl.ds(col0, 256)]
                spread = jnp.concatenate([query * m for m in head_mask], axis=0)
                scores = lax.dot_general(
                    keys, spread, (((1,), (1,)), ((), ())), preferred_element_type=F32
                )
                scores = scores * factor + bias[window, b]
                top = jnp.max(scores, axis=0, keepdims=True)
                raised = jnp.exp2(scores - top)
                total = jnp.sum(raised, axis=0, keepdims=True)
                weights = (raised * (1.0 / total)).astype(BF16)
                heads = lax.dot_general(
                    weights, values, (((0,), (0,)), ((), ())), preferred_element_type=F32
                )
                picked = jnp.zeros((16, 256), F32)
                for h in range(8):
                    picked = jnp.where(head_lane == h, heads[16 * h : 16 * h + 16], picked)
                att[rows, pl.ds(col0, 256)] = picked.astype(BF16)
            return carry

        lax.fori_loop(0, 4, attend, 0)
        loads[7 + g].wait()
        back[g][...] = dot(fromwin[g][...], att[...]).astype(BF16)
        copies = []
        for i, (begin, size) in enumerate(SEGMENTS[g]):
            rows = pl.ds(begin, size)
            copies.append(remote(4 + g + i, back[g].at[rows], home[g].at[rows], upper[i]))
            copies[-1].start()
        second.append(copies)

    for i in (9, 10, 11, 12, 13):
        loads[i].wait()
    for g in range(2):
        for copy in second[g]:
            copy.wait_recv()
        own = SEGMENTS[g][0][0]
        staged = jnp.concatenate([back[g][0:own], home[g][own:]], axis=0)
        attended = dot(tofinal[g][...], staged).astype(BF16)
        after = (resid[g] + dot(attended, wo[...])).astype(BF16)
        after_wide = after.astype(F32)
        normed = norm(after_wide, gm_ref[...], D).astype(BF16)
        total = after_wide
        for c in range(4):
            cols = slice(c * 512, c * 512 + 512)
            up = dot(normed, wup[:, cols])
            hidden = (0.5 * up * (1.0 + lax.erf(up * (2.0 ** -0.5)))).astype(BF16)
            total = total + dot(hidden, wdn[cols, :])
        done = total.astype(BF16).astype(F32)
        for pos in range(4):
            for jslot, j in enumerate(MERGE_COLS[g][pos // 2]):
                at = pos * 72 + jslot * 24
                joined[24 * j : 24 * j + 24, D * pos : D * pos + D] = done[at : at + 24]

    loads[14].wait()
    merged = dot(norm(joined[...], gg_ref[...], 4 * D).astype(BF16), wm[...])
    for j in range(6):
        tiles = merged[24 * j : 24 * j + 24].reshape(6, 4, MERGED).astype(BF16)
        for i in range(6):
            out_ref[i, j] = tiles[i]
    for copy in first + second[0] + second[1]:
        copy.wait_send()


def on_device(
    lat_count, lon_count, patches, w_query, w_keyval, w_out, w_up, w_down, w_merge,
    gain_attn, gain_mlp, gain_merge, lat_valid, region_ids,
):
    perms = [jnp.asarray(m) for m in permutations()]
    hbm = pl.BlockSpec(memory_space=pl.ANY)
    vmem = pl.BlockSpec(memory_space=pltpu.VMEM)
    smem = pl.BlockSpec(memory_space=pltpu.SMEM)
    grid = patches.transpose(1, 2, 0, 3)
    weights = (w_query, w_keyval, w_out, w_up, w_down, w_merge)
    held = [pltpu.VMEM(v.shape, v.dtype) for v in (grid,) + weights + tuple(perms)]
    merged = pl.pallas_call(
        functools.partial(kernel, lat_count, lon_count),
        out_shape=jax.ShapeDtypeStruct((6, 6, 4, MERGED), BF16),
        in_specs=[hbm] * 13 + [vmem] * 3 + [smem] * 2,
        out_specs=vmem,
        scratch_shapes=held
        + [
            pltpu.VMEM((12, 6, 4, D), BF16),
            pltpu.VMEM((12, 6, 4, D), BF16),
            pltpu.VMEM((BACK_ROWS[0], D), BF16),
            pltpu.VMEM((BACK_ROWS[1], D), BF16),
            pltpu.VMEM((BACK_ROWS[0], D), BF16),
            pltpu.VMEM((BACK_ROWS[1], D), BF16),
            pltpu.VMEM((4, CELLS, 128), F32),
            pltpu.VMEM((CELLS, 3 * D), BF16),
            pltpu.VMEM((CELLS, D), BF16),
            pltpu.VMEM((2, 9, WINDOW, 128), F32),
            pltpu.VMEM((2, CELLS, D), F32),
            pltpu.VMEM((144, 4 * D), F32),
            pltpu.SemaphoreType.DMA((15,)),
            pltpu.SemaphoreType.DMA((8,)),
            pltpu.SemaphoreType.DMA((8,)),
        ],
        compiler_params=pltpu.CompilerParams(
            collective_id=0, has_side_effects=True, vmem_limit_bytes=56 * 1024 * 1024
        ),
        cost_estimate=pl.CostEstimate(
            flops=6_000_000_000, bytes_accessed=12_000_000, transcendentals=3_000_000
        ),
    )(
        grid, *weights, *perms,
        gain_attn.reshape(1, -1), gain_mlp.reshape(1, -1), gain_merge.reshape(1, -1),
        lat_valid, region_ids,
    )
    return merged.transpose(2, 0, 1, 3)


def solution(mesh):
    placed = (P(None, "lat", "lon", None),) + (P(),) * 11
    return jax.shard_map(
        functools.partial(on_device, mesh.shape["lat"], mesh.shape["lon"]),
        mesh=mesh,
        in_specs=placed,
        out_specs=P(None, "lat", "lon", None),
        check_vma=False,
    )
```

```python
import functools
import math

import jax
import jax.numpy as jnp
import numpy as np
from jax import lax
from jax.experimental import pallas as pl
from jax.experimental.pallas import tpu as pltpu
from jax.sharding import PartitionSpec as P

HEADS = 16
D = 512
FFN = 2048
MERGED = 1024
WIN_LAT = 12
SHIFT_LAT = 6
EPSILON = 1e-05
MESH = pl.DeviceIdType.MESH
F32 = jnp.float32
BF16 = jnp.bfloat16

CELLS = 288
WINDOW = 144
LEVEL_SLOTS = (1, 2, 3, 0)
BACK_ROWS = (288, 320)
SEGMENTS = (((144, 144),), ((80, 80), (160, 80), (240, 80)))
MERGE_COLS = (((2, 3, 4), (1, 2, 3)), ((5, 0, 1), (4, 5, 0)))


def permutations():
    result = []
    for g in range(2):
        from_win = np.zeros((BACK_ROWS[g], CELLS), np.float32)
        to_final = np.zeros((CELLS, BACK_ROWS[g]), np.float32)
        flat_final = np.zeros((CELLS, 576), np.float32)
        for slot, lev in enumerate(LEVEL_SLOTS):
            for wr in range(12):
                for wc in range(6):
                    win = slot * 72 + wr * 6 + wc
                    if g == 0:
                        seg = (wr // 6) * 144 + slot * 36 + (wr % 6) * 6 + wc
                    else:
                        seg = (wr // 6 + 2 * (wc // 3)) * 80 + slot * 18 + (wr % 6) * 3 + wc % 3
                    row, col = (wr + 6) % 12, (wc + 3 + 6 * g) % 12
                    pos = row % 2 + 2 * (col % 2)
                    jslot = MERGE_COLS[g][col % 2].index(col // 2)
                    final = pos * 72 + jslot * 24 + (row // 2) * 4 + lev
                    from_win[seg, win] = 1
                    to_final[final, seg] = 1
                    flat_final[final, (row * 12 + col) * 4 + lev] = 1
        result += [from_win, to_final, flat_final]
    return [m.astype(jnp.bfloat16) for m in result]


def norm(wide, gain, width):
    average = jnp.sum(wide, axis=-1, keepdims=True) * (1.0 / width)
    centred = wide - average
    variance = jnp.sum(centred * centred, axis=-1, keepdims=True) * (1.0 / width)
    return centred * lax.rsqrt(variance + EPSILON) * gain


def dot(a, b):
    return jnp.dot(a, b, preferred_element_type=F32)


def kernel(
    lat_count,
    lon_count,
    x_hbm, wq_hbm, wkv_hbm, wo_hbm, wup_hbm, wdn_hbm, wm_hbm,
    fromwin0_hbm, tofinal0_hbm, flat0_hbm, fromwin1_hbm, tofinal1_hbm, flat1_hbm,
    ga_ref, gm_ref, gg_ref, valid_ref, region_ref,
    out_ref,
    x_v, wq, wkv, wo, wup, wdn, wm,
    fromwin0, tofinal0, flat0, fromwin1, tofinal1, flat1,
    cells0, cells1, back0, back1, home0, home1, wide, qkv, att, bias, resid, joined,
    local_sem, send_sem, recv_sem,
):
    a, o = lax.axis_index("lat"), lax.axis_index("lon")
    lat_dn = lax.rem(a + lat_count - 1, lat_count)
    lat_up = lax.rem(a + 1, lat_count)
    lon_dn = lax.rem(o + lon_count - 1, lon_count)
    lon_up = lax.rem(o + 1, lon_count)
    lower = ((lat_dn, o), (a, lon_dn), (lat_dn, lon_dn))
    upper = ((lat_up, o), (a, lon_up), (lat_up, lon_up))
    cells, back, home = (cells0, cells1), (back0, back1), (home0, home1)
    fromwin, tofinal, flat = (fromwin0, fromwin1), (tofinal0, tofinal1), (flat0, flat1)

    barrier = pltpu.get_barrier_semaphore()
    for device in lower + upper:
        pl.semaphore_signal(barrier, inc=1, device_id=device, device_id_type=MESH)

    pairs = (
        (x_hbm.at[pl.ds(6, 6), pl.ds(3, 6)], cells0.at[pl.ds(0, 6)]),
        (x_hbm.at[pl.ds(6, 6), pl.ds(9, 3)], cells1.at[pl.ds(0, 6), pl.ds(0, 3)]),
        (x_hbm, x_v), (wq_hbm, wq), (wkv_hbm, wkv), (flat0_hbm, flat0), (flat1_hbm, flat1),
        (fromwin0_hbm, fromwin0), (fromwin1_hbm, fromwin1),
        (tofinal0_hbm, tofinal0), (tofinal1_hbm, tofinal1),
        (wo_hbm, wo), (wup_hbm, wup), (wdn_hbm, wdn), (wm_hbm, wm),
    )
    loads = [pltpu.make_async_copy(s, d, local_sem.at[i]) for i, (s, d) in enumerate(pairs)]

    def remote(slot, source, target, device):
        return pltpu.make_async_remote_copy(
            src_ref=source, dst_ref=target, send_sem=send_sem.at[slot], recv_sem=recv_sem.at[slot],
            device_id=device, device_id_type=MESH,
        )

    first = [
        remote(0, x_hbm.at[pl.ds(0, 6), pl.ds(3, 6)], cells0.at[pl.ds(6, 6)], lower[0]),
        remote(1, x_hbm.at[pl.ds(0, 6), pl.ds(0, 3)], cells1.at[pl.ds(6, 6), pl.ds(3, 3)], lower[2]),
        remote(2, x_hbm.at[pl.ds(6, 6), pl.ds(0, 3)], cells1.at[pl.ds(0, 6), pl.ds(3, 3)], lower[1]),
        remote(3, x_hbm.at[pl.ds(0, 6), pl.ds(9, 3)], cells1.at[pl.ds(6, 6), pl.ds(0, 3)], lower[0]),
    ]
    for load in loads[:3]:
        load.start()
    pl.semaphore_wait(barrier, 6)
    for copy in first:
        copy.start()
    for load in loads[3:]:
        load.start()

    key_row = lax.broadcasted_iota(jnp.int32, (WINDOW, 128), 0)
    key_lev = (key_row >= 72).astype(jnp.int32)
    key_lat = ((key_row - 72 * key_lev) * 683) >> 12
    start = a * WIN_LAT + SHIFT_LAT
    row_ids = [lax.rem(start + r, lat_count * WIN_LAT) for r in range(WIN_LAT)]
    tags = [region_ref[i] for i in row_ids]
    valid = [valid_ref[i] for i in row_ids]
    key_tag = jnp.zeros((WINDOW, 128), jnp.int32)
    key_valid = jnp.zeros((WINDOW, 128), jnp.int32)
    for r in range(WIN_LAT):
        key_tag = jnp.where(key_lat == r, tags[r], key_tag)
        key_valid = jnp.where(key_lat == r, valid[r], key_valid)
    lane = lax.broadcasted_iota(jnp.int32, (1, 128), 1) & 15
    for b in range(9):
        query = lane + 16 * b
        query_lev = (query >= 72).astype(jnp.int32)
        query_lat = ((query - 72 * query_lev) * 683) >> 12
        query_tag = jnp.zeros((1, 128), jnp.int32)
        for r in range(WIN_LAT):
            query_tag = jnp.where(query_lat == r, tags[r], query_tag)
        usable = (key_tag == query_tag) & ((key_valid == 1) | (key_row == query))
        bias[0, b] = jnp.where(usable, 0.0, -jnp.inf)
        bias[1, b] = jnp.where(usable & (key_lev == query_lev), 0.0, -jnp.inf)

    for i in (2, 5, 6):
        loads[i].wait()
    mine = jnp.concatenate([x_v[r].astype(F32).reshape(48, D) for r in range(12)], axis=0).astype(BF16)
    for g in range(2):
        resid[g] = dot(flat[g][...], mine)

    head_lane = lax.broadcasted_iota(jnp.int32, (16, 256), 1) >> 5
    head_mask = [(head_lane == h).astype(F32).astype(BF16) for h in range(8)]
    factor = math.log2(math.e) / math.sqrt(D // HEADS)

    second = []
    for g in range(2):
        loads[g].wait()
        for copy in (first[:1], first[1:])[g]:
            copy.wait_recv()
        if g == 0:
            loads[3].wait()
            loads[4].wait()
        for row in range(12):
            flat_row = cells[g][row].astype(F32).reshape(24, D)
            for c in range(4):
                wide[c, 24 * row : 24 * row + 24, :] = flat_row[:, 128 * c : 128 * c + 128]
        levels = [
            jnp.concatenate([wide[c, pl.ds(lev, 72, stride=4), :] for c in range(4)], axis=1)
            for lev in LEVEL_SLOTS
        ]
        normed = norm(jnp.concatenate(levels, axis=0), ga_ref[...], D).astype(BF16)
        qkv[:, 0:D] = dot(normed, wq[...]).astype(BF16)
        qkv[:, D : 3 * D] = dot(normed, wkv[...]).astype(BF16)

        def attend(step, carry):
            window = step // 2
            row0 = pl.multiple_of(window * WINDOW, 16)
            col0 = pl.multiple_of((step % 2) * 256, 256)
            keys = qkv[pl.ds(row0, WINDOW), pl.ds(pl.multiple_of(D + col0, 256), 256)]
            values = qkv[pl.ds(row0, WINDOW), pl.ds(pl.multiple_of(2 * D + col0, 256), 256)]
            scores, weights, heads = [], [], []
            for b in range(9):
                query = qkv[pl.ds(pl.multiple_of(row0 + 16 * b, 16), 16), pl.ds(col0, 256)]
                spread = jnp.concatenate([query * m for m in head_mask], axis=0)
                scores.append(
                    lax.dot_general(
                        keys, spread, (((1,), (1,)), ((), ())), preferred_element_type=F32
                    )
                )
            for b in range(9):
                logits = scores[b] * factor + bias[window, b]
                top = jnp.max(logits, axis=0, keepdims=True)
                raised = jnp.exp2(logits - top)
                total = jnp.sum(raised, axis=0, keepdims=True)
                weights.append((raised * (1.0 / total)).astype(BF16))
            for b in range(9):
                heads.append(
                    lax.dot_general(
                        weights[b], values, (((0,), (0,)), ((), ())), preferred_element_type=F32
                    )
                )
            for b in range(9):
                picked = jnp.zeros((16, 256), F32)
                for h in range(8):
                    picked = jnp.where(head_lane == h, heads[b][16 * h : 16 * h + 16], picked)
                rows = pl.ds(pl.multiple_of(row0 + 16 * b, 16), 16)
                att[rows, pl.ds(col0, 256)] = picked.astype(BF16)
            return carry

        lax.fori_loop(0, 4, attend, 0, unroll=4)
        loads[7 + g].wait()
        back[g][...] = dot(fromwin[g][...], att[...]).astype(BF16)
        copies = []
        for i, (begin, size) in enumerate(SEGMENTS[g]):
            rows = pl.ds(begin, size)
            copies.append(remote(4 + g + i, back[g].at[rows], home[g].at[rows], upper[i]))
            copies[-1].start()
        second.append(copies)

    for i in (9, 10, 11, 12, 13):
        loads[i].wait()
    for g in range(2):
        for copy in second[g]:
            copy.wait_recv()
        own = SEGMENTS[g][0][0]
        staged = jnp.concatenate([back[g][0:own], home[g][own:]], axis=0)
        attended = dot(tofinal[g][...], staged).astype(BF16)
        after = (resid[g] + dot(attended, wo[...])).astype(BF16)
        after_wide = after.astype(F32)
        normed = norm(after_wide, gm_ref[...], D).astype(BF16)
        total = after_wide
        for c in range(4):
            cols = slice(c * 512, c * 512 + 512)
            up = dot(normed, wup[:, cols])
            hidden = (0.5 * up * (1.0 + lax.erf(up * (2.0 ** -0.5)))).astype(BF16)
            total = total + dot(hidden, wdn[cols, :])
        done = total.astype(BF16).astype(F32)
        for pos in range(4):
            for jslot, j in enumerate(MERGE_COLS[g][pos // 2]):
                at = pos * 72 + jslot * 24
                joined[24 * j : 24 * j + 24, D * pos : D * pos + D] = done[at : at + 24]

    loads[14].wait()
    merged = dot(norm(joined[...], gg_ref[...], 4 * D).astype(BF16), wm[...])
    for j in range(6):
        tiles = merged[24 * j : 24 * j + 24].reshape(6, 4, MERGED).astype(BF16)
        for i in range(6):
            out_ref[i, j] = tiles[i]
    for copy in first + second[0] + second[1]:
        copy.wait_send()


def on_device(
    lat_count, lon_count, patches, w_query, w_keyval, w_out, w_up, w_down, w_merge,
    gain_attn, gain_mlp, gain_merge, lat_valid, region_ids,
):
    perms = [jnp.asarray(m) for m in permutations()]
    hbm = pl.BlockSpec(memory_space=pl.ANY)
    vmem = pl.BlockSpec(memory_space=pltpu.VMEM)
    smem = pl.BlockSpec(memory_space=pltpu.SMEM)
    grid = patches.transpose(1, 2, 0, 3)
    weights = (w_query, w_keyval, w_out, w_up, w_down, w_merge)
    held = [pltpu.VMEM(v.shape, v.dtype) for v in (grid,) + weights + tuple(perms)]
    merged = pl.pallas_call(
        functools.partial(kernel, lat_count, lon_count),
        out_shape=jax.ShapeDtypeStruct((6, 6, 4, MERGED), BF16),
        in_specs=[hbm] * 13 + [vmem] * 3 + [smem] * 2,
        out_specs=vmem,
        scratch_shapes=held
        + [
            pltpu.VMEM((12, 6, 4, D), BF16),
            pltpu.VMEM((12, 6, 4, D), BF16),
            pltpu.VMEM((BACK_ROWS[0], D), BF16),
            pltpu.VMEM((BACK_ROWS[1], D), BF16),
            pltpu.VMEM((BACK_ROWS[0], D), BF16),
            pltpu.VMEM((BACK_ROWS[1], D), BF16),
            pltpu.VMEM((4, CELLS, 128), F32),
            pltpu.VMEM((CELLS, 3 * D), BF16),
            pltpu.VMEM((CELLS, D), BF16),
            pltpu.VMEM((2, 9, WINDOW, 128), F32),
            pltpu.VMEM((2, CELLS, D), F32),
            pltpu.VMEM((144, 4 * D), F32),
            pltpu.SemaphoreType.DMA((15,)),
            pltpu.SemaphoreType.DMA((8,)),
            pltpu.SemaphoreType.DMA((8,)),
        ],
        compiler_params=pltpu.CompilerParams(
            collective_id=0, has_side_effects=True, vmem_limit_bytes=56 * 1024 * 1024
        ),
        cost_estimate=pl.CostEstimate(
            flops=6_000_000_000, bytes_accessed=12_000_000, transcendentals=3_000_000
        ),
    )(
        grid, *weights, *perms,
        gain_attn.reshape(1, -1), gain_mlp.reshape(1, -1), gain_merge.reshape(1, -1),
        lat_valid, region_ids,
    )
    return merged.transpose(2, 0, 1, 3)


def solution(mesh):
    placed = (P(None, "lat", "lon", None),) + (P(),) * 11
    return jax.shard_map(
        functools.partial(on_device, mesh.shape["lat"], mesh.shape["lon"]),
        mesh=mesh,
        in_specs=placed,
        out_specs=P(None, "lat", "lon", None),
        check_vma=False,
    )
```

```python
import functools
import math

import jax
import jax.numpy as jnp
import numpy as np
from jax import lax
from jax.experimental import pallas as pl
from jax.experimental.pallas import tpu as pltpu
from jax.sharding import PartitionSpec as P

HEADS = 16
D = 512
FFN = 2048
MERGED = 1024
WIN_LAT = 12
SHIFT_LAT = 6
EPSILON = 1e-05
MESH = pl.DeviceIdType.MESH
F32 = jnp.float32
BF16 = jnp.bfloat16

CELLS = 288
WINDOW = 144
LEVEL_SLOTS = (1, 2, 3, 0)
BACK_ROWS = (288, 320)
MERGE_COLS = (((2, 3, 4), (1, 2, 3)), ((5, 0, 1), (4, 5, 0)))


def permutations():
    result = []
    for g in range(2):
        from_win = np.zeros((BACK_ROWS[g], CELLS), np.float32)
        to_final = np.zeros((CELLS, BACK_ROWS[g]), np.float32)
        flat_final = np.zeros((CELLS, 576), np.float32)
        for slot, lev in enumerate(LEVEL_SLOTS):
            for wr in range(12):
                for wc in range(6):
                    win = slot * 72 + wr * 6 + wc
                    if g == 0:
                        seg = (wr // 6) * 144 + slot * 36 + (wr % 6) * 6 + wc
                    else:
                        part = wr // 6 + 2 * (wc // 3)
                        seg = (slot // 2) * 160 + part * 40 + (slot % 2) * 18 + (wr % 6) * 3 + wc % 3
                    row, col = (wr + 6) % 12, (wc + 3 + 6 * g) % 12
                    pos = row % 2 + 2 * (col % 2)
                    jslot = MERGE_COLS[g][col % 2].index(col // 2)
                    final = pos * 72 + jslot * 24 + (row // 2) * 4 + lev
                    from_win[seg, win] = 1
                    to_final[final, seg] = 1
                    flat_final[final, (row * 12 + col) * 4 + lev] = 1
        result += [from_win[0:160, 0:144] if g else from_win, to_final, flat_final]
    return [m.astype(jnp.bfloat16) for m in result]


def norm(wide, gain, width):
    average = jnp.sum(wide, axis=-1, keepdims=True) * (1.0 / width)
    centred = wide - average
    variance = jnp.sum(centred * centred, axis=-1, keepdims=True) * (1.0 / width)
    return centred * lax.rsqrt(variance + EPSILON) * gain


def dot(a, b):
    return jnp.dot(a, b, preferred_element_type=F32)


def kernel(
    lat_count,
    lon_count,
    x_hbm, wq_hbm, wkv_hbm, wo_hbm, wup_hbm, wdn_hbm, wm_hbm,
    fromwin0_hbm, tofinal0_hbm, flat0_hbm, fromwin1_hbm, tofinal1_hbm, flat1_hbm,
    ga_hbm, gm_hbm, gg_hbm, valid_hbm, region_hbm,
    out_ref,
    x_v, wq, wkv, wo, wup, wdn, wm,
    fromwin0, tofinal0, flat0, fromwin1, tofinal1, flat1,
    ga_ref, gm_ref, gg_ref, valid_ref, region_ref,
    cells0, cells1, back0, back1, home0, home1, wide, qkv, att, bias, resid, joined,
    local_sem, send_sem, recv_sem,
):
    a, o = lax.axis_index("lat"), lax.axis_index("lon")
    lat_dn = lax.rem(a + lat_count - 1, lat_count)
    lat_up = lax.rem(a + 1, lat_count)
    lon_dn = lax.rem(o + lon_count - 1, lon_count)
    lon_up = lax.rem(o + 1, lon_count)
    lower = ((lat_dn, o), (a, lon_dn), (lat_dn, lon_dn))
    upper = ((lat_up, o), (a, lon_up), (lat_up, lon_up))
    cells, tofinal, flat = (cells0, cells1), (tofinal0, tofinal1), (flat0, flat1)

    barrier = pltpu.get_barrier_semaphore()
    for device in lower + upper:
        pl.semaphore_signal(barrier, inc=1, device_id=device, device_id_type=MESH)

    pairs = (
        (x_hbm.at[pl.ds(6, 6), pl.ds(3, 6)], cells0.at[pl.ds(0, 6)]),
        (x_hbm.at[pl.ds(6, 6), pl.ds(9, 3)], cells1.at[pl.ds(0, 6), pl.ds(0, 3)]),
        (x_hbm, x_v), (wq_hbm, wq), (wkv_hbm, wkv), (flat0_hbm, flat0), (flat1_hbm, flat1),
        (fromwin0_hbm, fromwin0), (fromwin1_hbm, fromwin1),
        (tofinal0_hbm, tofinal0), (tofinal1_hbm, tofinal1),
        (wo_hbm, wo), (wup_hbm, wup), (wdn_hbm, wdn), (wm_hbm, wm),
        (region_hbm, region_ref), (valid_hbm, valid_ref),
        (ga_hbm, ga_ref), (gm_hbm, gm_ref), (gg_hbm, gg_ref),
    )
    loads = [pltpu.make_async_copy(s, d, local_sem.at[i]) for i, (s, d) in enumerate(pairs)]

    def remote(slot, source, target, device):
        return pltpu.make_async_remote_copy(
            src_ref=source, dst_ref=target, send_sem=send_sem.at[slot], recv_sem=recv_sem.at[slot],
            device_id=device, device_id_type=MESH,
        )

    first = [
        remote(0, x_hbm.at[pl.ds(0, 6), pl.ds(3, 6)], cells0.at[pl.ds(6, 6)], lower[0]),
        remote(1, x_hbm.at[pl.ds(0, 6), pl.ds(0, 3)], cells1.at[pl.ds(6, 6), pl.ds(3, 3)], lower[2]),
        remote(2, x_hbm.at[pl.ds(6, 6), pl.ds(0, 3)], cells1.at[pl.ds(0, 6), pl.ds(3, 3)], lower[1]),
        remote(3, x_hbm.at[pl.ds(0, 6), pl.ds(9, 3)], cells1.at[pl.ds(6, 6), pl.ds(0, 3)], lower[0]),
    ]
    for load in loads[15:17] + loads[:3]:
        load.start()
    pl.semaphore_wait(barrier, 6)
    for copy in first:
        copy.start()
    for load in loads[17:] + loads[3:15]:
        load.start()

    key_row = lax.broadcasted_iota(jnp.int32, (WINDOW, 128), 0)
    key_lev = (key_row >= 72).astype(jnp.int32)
    key_lat = ((key_row - 72 * key_lev) * 683) >> 12
    start = a * WIN_LAT + SHIFT_LAT
    loads[15].wait()
    loads[16].wait()
    row_ids = [lax.rem(start + r, lat_count * WIN_LAT) for r in range(WIN_LAT)]
    tags = [region_ref[i] for i in row_ids]
    valid = [valid_ref[i] for i in row_ids]
    key_tag = jnp.zeros((WINDOW, 128), jnp.int32)
    key_valid = jnp.zeros((WINDOW, 128), jnp.int32)
    for r in range(WIN_LAT):
        key_tag = jnp.where(key_lat == r, tags[r], key_tag)
        key_valid = jnp.where(key_lat == r, valid[r], key_valid)
    lane = lax.broadcasted_iota(jnp.int32, (1, 128), 1) & 15
    for b in range(9):
        query = lane + 16 * b
        query_lev = (query >= 72).astype(jnp.int32)
        query_lat = ((query - 72 * query_lev) * 683) >> 12
        query_tag = jnp.zeros((1, 128), jnp.int32)
        for r in range(WIN_LAT):
            query_tag = jnp.where(query_lat == r, tags[r], query_tag)
        usable = (key_tag == query_tag) & ((key_valid == 1) | (key_row == query))
        bias[0, b] = jnp.where(usable, 0.0, -jnp.inf)
        bias[1, b] = jnp.where(usable & (key_lev == query_lev), 0.0, -jnp.inf)

    first[0].wait_send()

    for i in (2, 5, 6, 17):
        loads[i].wait()
    mine = jnp.concatenate([x_v[r].astype(F32).reshape(48, D) for r in range(12)], axis=0).astype(BF16)
    for g in range(2):
        resid[g] = dot(flat[g][...], mine)

    head_lane = lax.broadcasted_iota(jnp.int32, (16, 256), 1) >> 5
    head_mask = [(head_lane == h).astype(F32).astype(BF16) for h in range(8)]
    factor = math.log2(math.e) / math.sqrt(D // HEADS)

    second = []
    for g in range(2):
        loads[g].wait()
        for copy in (first[:1], first[1:])[g]:
            copy.wait_recv()
        if g == 0:
            loads[3].wait()
            loads[4].wait()
        for row in range(12):
            flat_row = cells[g][row].astype(F32).reshape(24, D)
            for c in range(4):
                wide[c, 24 * row : 24 * row + 24, :] = flat_row[:, 128 * c : 128 * c + 128]
        levels = [
            jnp.concatenate([wide[c, pl.ds(lev, 72, stride=4), :] for c in range(4)], axis=1)
            for lev in LEVEL_SLOTS
        ]
        normed = norm(jnp.concatenate(levels, axis=0), ga_ref[...], D).astype(BF16)
        qkv[:, 0:D] = dot(normed, wq[...]).astype(BF16)
        qkv[:, D : 3 * D] = dot(normed, wkv[...]).astype(BF16)

        def attend(window, half):
            row0, col0 = window * WINDOW, half * 256
            keys = qkv[row0 : row0 + WINDOW, D + col0 : D + col0 + 256]
            values = qkv[row0 : row0 + WINDOW, 2 * D + col0 : 2 * D + col0 + 256]
            scores, weights, heads = [], [], []
            for b in range(9):
                query = qkv[row0 + 16 * b : row0 + 16 * b + 16, col0 : col0 + 256]
                spread = jnp.concatenate([query * m for m in head_mask], axis=0)
                scores.append(
                    lax.dot_general(
                        keys, spread, (((1,), (1,)), ((), ())), preferred_element_type=F32
                    )
                )
            for b in range(9):
                logits = scores[b] * factor + bias[window, b]
                top = jnp.max(logits, axis=0, keepdims=True)
                raised = jnp.exp2(logits - top)
                total = jnp.sum(raised, axis=0, keepdims=True)
                weights.append((raised * (1.0 / total)).astype(BF16))
            for b in range(9):
                heads.append(
                    lax.dot_general(
                        weights[b], values, (((0,), (0,)), ((), ())), preferred_element_type=F32
                    )
                )
            for b in range(9):
                picked = jnp.zeros((16, 256), F32)
                for h in range(8):
                    picked = jnp.where(head_lane == h, heads[b][16 * h : 16 * h + 16], picked)
                at = row0 + 16 * b
                att[at : at + 16, col0 : col0 + 256] = picked.astype(BF16)

        if g == 0:
            for window in range(2):
                for half in range(2):
                    attend(window, half)
            loads[7].wait()
            back0[...] = dot(fromwin0[...], att[...]).astype(BF16)
            rows = pl.ds(144, 144)
            second.append([remote(4, back0.at[rows], home0.at[rows], upper[0])])
            second[0][0].start()
        else:
            loads[8].wait()
            second.append([])
            for window in range(2):
                for half in range(2):
                    attend(window, half)
                moved = dot(fromwin1[...], att[window * WINDOW : window * WINDOW + WINDOW, :])
                back1[window] = moved.reshape(20, 8, D).astype(BF16)
                for i in range(3):
                    part = (window, pl.ds(5 * i + 5, 5))
                    copy = remote(5 + 3 * window + i, back1.at[part], home1.at[part], upper[i])
                    copy.start()
                    second[1].append(copy)

    for i in (9, 10, 11, 12, 13, 18, 19):
        loads[i].wait()
    for g in range(2):
        for copy in second[g]:
            copy.wait_recv()
        if g == 0:
            staged = jnp.concatenate([back0[0:144], home0[144:]], axis=0)
        else:
            parts = [r for w in range(2) for r in (back1[w, 0:5], home1[w, 5:20])]
            staged = jnp.concatenate([r.astype(F32).reshape(-1, D) for r in parts], axis=0).astype(BF16)
        attended = dot(tofinal[g][...], staged).astype(BF16)
        after = (resid[g] + dot(attended, wo[...])).astype(BF16)
        after_wide = after.astype(F32)
        normed = norm(after_wide, gm_ref[...], D).astype(BF16)
        total = after_wide
        for c in range(2):
            cols = slice(c * 1024, c * 1024 + 1024)
            up = dot(normed, wup[:, cols])
            hidden = (0.5 * up * (1.0 + lax.erf(up * (2.0 ** -0.5)))).astype(BF16)
            total = total + dot(hidden, wdn[cols, :])
        done = total.astype(BF16).astype(F32)
        for pos in range(4):
            for jslot, j in enumerate(MERGE_COLS[g][pos // 2]):
                at = pos * 72 + jslot * 24
                joined[24 * j : 24 * j + 24, D * pos : D * pos + D] = done[at : at + 24]

    loads[14].wait()
    merged = dot(norm(joined[...], gg_ref[...], 4 * D).astype(BF16), wm[...])
    for j in range(6):
        tiles = merged[24 * j : 24 * j + 24].reshape(6, 4, MERGED).astype(BF16)
        for i in range(6):
            out_ref[i, j] = tiles[i]
    for copy in first[1:] + second[0] + second[1]:
        copy.wait_send()


def on_device(
    lat_count, lon_count, patches, w_query, w_keyval, w_out, w_up, w_down, w_merge,
    gain_attn, gain_mlp, gain_merge, lat_valid, region_ids,
):
    perms = [jnp.asarray(m) for m in permutations()]
    hbm = pl.BlockSpec(memory_space=pl.ANY)
    vmem = pl.BlockSpec(memory_space=pltpu.VMEM)
    grid = patches.transpose(1, 2, 0, 3)
    weights = (w_query, w_keyval, w_out, w_up, w_down, w_merge)
    held = [pltpu.VMEM(v.shape, v.dtype) for v in (grid,) + weights + tuple(perms)]
    merged = pl.pallas_call(
        functools.partial(kernel, lat_count, lon_count),
        out_shape=pltpu.VMEM((6, 6, 4, MERGED), BF16),
        in_specs=[hbm] * 18,
        out_specs=vmem,
        scratch_shapes=held
        + [
            pltpu.VMEM((1, D), F32),
            pltpu.VMEM((1, D), F32),
            pltpu.VMEM((1, 4 * D), F32),
            pltpu.SMEM(lat_valid.shape, jnp.int32),
            pltpu.SMEM(region_ids.shape, jnp.int32),
            pltpu.VMEM((12, 6, 4, D), BF16),
            pltpu.VMEM((12, 6, 4, D), BF16),
            pltpu.VMEM((BACK_ROWS[0], D), BF16),
            pltpu.VMEM((2, 20, 8, D), BF16),
            pltpu.VMEM((BACK_ROWS[0], D), BF16),
            pltpu.VMEM((2, 20, 8, D), BF16),
            pltpu.VMEM((4, CELLS, 128), F32),
            pltpu.VMEM((CELLS, 3 * D), BF16),
            pltpu.VMEM((CELLS, D), BF16),
            pltpu.VMEM((2, 9, WINDOW, 128), F32),
            pltpu.VMEM((2, CELLS, D), F32),
            pltpu.VMEM((144, 4 * D), F32),
            pltpu.SemaphoreType.DMA((20,)),
            pltpu.SemaphoreType.DMA((11,)),
            pltpu.SemaphoreType.DMA((11,)),
        ],
        compiler_params=pltpu.CompilerParams(
            collective_id=0, has_side_effects=True, vmem_limit_bytes=56 * 1024 * 1024
        ),
        cost_estimate=pl.CostEstimate(
            flops=6_000_000_000, bytes_accessed=12_000_000, transcendentals=3_000_000
        ),
    )(
        grid, *weights, *perms,
        gain_attn.reshape(1, -1), gain_mlp.reshape(1, -1), gain_merge.reshape(1, -1),
        lat_valid, region_ids,
    )
    return merged.transpose(2, 0, 1, 3)


def solution(mesh):
    placed = (P(None, "lat", "lon", None),) + (P(),) * 11
    return jax.shard_map(
        functools.partial(on_device, mesh.shape["lat"], mesh.shape["lon"]),
        mesh=mesh,
        in_specs=placed,
        out_specs=P(None, "lat", "lon", None),
        check_vma=False,
    )
```

```python
import functools
import math

import jax
import jax.numpy as jnp
import numpy as np
from jax import lax
from jax.experimental import pallas as pl
from jax.experimental.pallas import tpu as pltpu
from jax.sharding import PartitionSpec as P

HEADS = 16
D = 512
FFN = 2048
MERGED = 1024
WIN_LAT = 12
SHIFT_LAT = 6
EPSILON = 1e-05
MESH = pl.DeviceIdType.MESH
F32 = jnp.float32
BF16 = jnp.bfloat16

CELLS = 288
WINDOW = 144
LEVEL_SLOTS = (1, 2, 3, 0)
BACK_ROWS = (288, 320)
MERGE_COLS = (((2, 3, 4), (1, 2, 3)), ((5, 0, 1), (4, 5, 0)))


def permutations():
    result = []
    for g in range(2):
        from_win = np.zeros((BACK_ROWS[g], CELLS), np.float32)
        to_final = np.zeros((CELLS, BACK_ROWS[g]), np.float32)
        flat_final = np.zeros((CELLS, 576), np.float32)
        for slot, lev in enumerate(LEVEL_SLOTS):
            for wr in range(12):
                for wc in range(6):
                    win = slot * 72 + wr * 6 + wc
                    if g == 0:
                        seg = (wr // 6) * 144 + slot * 36 + (wr % 6) * 6 + wc
                    else:
                        part = wr // 6 + 2 * (wc // 3)
                        seg = (slot // 2) * 160 + part * 40 + (slot % 2) * 18 + (wr % 6) * 3 + wc % 3
                    row, col = (wr + 6) % 12, (wc + 3 + 6 * g) % 12
                    pos = row % 2 + 2 * (col % 2)
                    jslot = MERGE_COLS[g][col % 2].index(col // 2)
                    final = pos * 72 + jslot * 24 + (row // 2) * 4 + lev
                    from_win[seg, win] = 1
                    to_final[final, seg] = 1
                    flat_final[final, (row * 12 + col) * 4 + lev] = 1
        result += [from_win[0:160, 0:144] if g else from_win, to_final, flat_final]
    return [m.astype(jnp.bfloat16) for m in result]


def norm(wide, gain, width):
    average = jnp.sum(wide, axis=-1, keepdims=True) * (1.0 / width)
    centred = wide - average
    variance = jnp.sum(centred * centred, axis=-1, keepdims=True) * (1.0 / width)
    return centred * lax.rsqrt(variance + EPSILON) * gain


def dot(a, b):
    return jnp.dot(a, b, preferred_element_type=F32)


def kernel(
    lat_count,
    lon_count,
    x_hbm, wq_hbm, wkv_hbm, wo_hbm, wup_hbm, wdn_hbm, wm_hbm,
    fromwin0_hbm, tofinal0_hbm, flat0_hbm, fromwin1_hbm, tofinal1_hbm, flat1_hbm,
    ga_hbm, gm_hbm, gg_hbm, valid_hbm, region_hbm,
    out_ref,
    x_v, wq, wkv, wo, wup, wdn, wm,
    fromwin0, tofinal0, flat0, fromwin1, tofinal1, flat1,
    ga_ref, gm_ref, gg_ref, valid_ref, region_ref,
    cells0, cells1, back0, back1, home0, home1, wide, qkv, att, bias, resid, joined,
    local_sem, send_sem, recv_sem,
):
    a, o = lax.axis_index("lat"), lax.axis_index("lon")
    lat_dn = lax.rem(a + lat_count - 1, lat_count)
    lat_up = lax.rem(a + 1, lat_count)
    lon_dn = lax.rem(o + lon_count - 1, lon_count)
    lon_up = lax.rem(o + 1, lon_count)
    lower = ((lat_dn, o), (a, lon_dn), (lat_dn, lon_dn))
    upper = ((lat_up, o), (a, lon_up), (lat_up, lon_up))
    cells, tofinal, flat = (cells0, cells1), (tofinal0, tofinal1), (flat0, flat1)

    barrier = pltpu.get_barrier_semaphore()
    for device in upper:
        pl.semaphore_signal(barrier, inc=1, device_id=device, device_id_type=MESH)

    pairs = (
        (x_hbm.at[pl.ds(6, 6), pl.ds(3, 6)], cells0.at[pl.ds(0, 6)]),
        (x_hbm.at[pl.ds(6, 6), pl.ds(9, 3)], cells1.at[pl.ds(0, 6), pl.ds(0, 3)]),
        (x_hbm, x_v), (wq_hbm, wq), (wkv_hbm, wkv), (flat0_hbm, flat0), (flat1_hbm, flat1),
        (fromwin0_hbm, fromwin0), (fromwin1_hbm, fromwin1),
        (tofinal0_hbm, tofinal0), (tofinal1_hbm, tofinal1),
        (wo_hbm, wo), (wup_hbm, wup), (wdn_hbm, wdn), (wm_hbm, wm),
        (region_hbm, region_ref), (valid_hbm, valid_ref),
        (ga_hbm, ga_ref), (gm_hbm, gm_ref), (gg_hbm, gg_ref),
    )
    loads = [pltpu.make_async_copy(s, d, local_sem.at[i]) for i, (s, d) in enumerate(pairs)]

    def remote(slot, source, target, device):
        return pltpu.make_async_remote_copy(
            src_ref=source, dst_ref=target, send_sem=send_sem.at[slot], recv_sem=recv_sem.at[slot],
            device_id=device, device_id_type=MESH,
        )

    first = [
        remote(0, x_hbm.at[pl.ds(0, 6), pl.ds(3, 6)], cells0.at[pl.ds(6, 6)], lower[0]),
        remote(1, x_hbm.at[pl.ds(0, 6), pl.ds(0, 3)], cells1.at[pl.ds(6, 6), pl.ds(3, 3)], lower[2]),
        remote(2, x_hbm.at[pl.ds(6, 6), pl.ds(0, 3)], cells1.at[pl.ds(0, 6), pl.ds(3, 3)], lower[1]),
        remote(3, x_hbm.at[pl.ds(0, 6), pl.ds(9, 3)], cells1.at[pl.ds(6, 6), pl.ds(0, 3)], lower[0]),
    ]
    for load in loads[15:17] + loads[:3]:
        load.start()
    pl.semaphore_wait(barrier, 3)
    for copy in first:
        copy.start()
    for load in loads[17:] + loads[3:15]:
        load.start()

    key_row = lax.broadcasted_iota(jnp.int32, (WINDOW, 128), 0)
    key_lev = (key_row >= 72).astype(jnp.int32)
    key_lat = ((key_row - 72 * key_lev) * 683) >> 12
    start = a * WIN_LAT + SHIFT_LAT
    loads[15].wait()
    loads[16].wait()
    row_ids = [lax.rem(start + r, lat_count * WIN_LAT) for r in range(WIN_LAT)]
    tags = [region_ref[i] for i in row_ids]
    valid = [valid_ref[i] for i in row_ids]
    key_tag = jnp.zeros((WINDOW, 128), jnp.int32)
    key_valid = jnp.zeros((WINDOW, 128), jnp.int32)
    for r in range(WIN_LAT):
        key_tag = jnp.where(key_lat == r, tags[r], key_tag)
        key_valid = jnp.where(key_lat == r, valid[r], key_valid)
    lane = lax.broadcasted_iota(jnp.int32, (1, 128), 1) & 15
    for b in range(9):
        query = lane + 16 * b
        query_lev = (query >= 72).astype(jnp.int32)
        query_lat = ((query - 72 * query_lev) * 683) >> 12
        query_tag = jnp.zeros((1, 128), jnp.int32)
        for r in range(WIN_LAT):
            query_tag = jnp.where(query_lat == r, tags[r], query_tag)
        usable = (key_tag == query_tag) & ((key_valid == 1) | (key_row == query))
        bias[0, b] = jnp.where(usable, 0.0, -jnp.inf)
        bias[1, b] = jnp.where(usable & (key_lev == query_lev), 0.0, -jnp.inf)

    first[0].wait_send()

    for i in (2, 5, 6, 17):
        loads[i].wait()
    mine = jnp.concatenate([x_v[r].astype(F32).reshape(48, D) for r in range(12)], axis=0).astype(BF16)
    for g in range(2):
        resid[g] = dot(flat[g][...], mine)

    head_lane = lax.broadcasted_iota(jnp.int32, (16, 256), 1) >> 5
    head_mask = [(head_lane == h).astype(F32).astype(BF16) for h in range(8)]
    factor = math.log2(math.e) / math.sqrt(D // HEADS)

    second = []
    for g in range(2):
        loads[g].wait()
        for copy in (first[:1], first[1:])[g]:
            copy.wait_recv()
        if g == 0:
            loads[3].wait()
            loads[4].wait()
        for row in range(12):
            flat_row = cells[g][row].astype(F32).reshape(24, D)
            for c in range(4):
                wide[c, 24 * row : 24 * row + 24, :] = flat_row[:, 128 * c : 128 * c + 128]
        levels = [
            jnp.concatenate([wide[c, pl.ds(lev, 72, stride=4), :] for c in range(4)], axis=1)
            for lev in LEVEL_SLOTS
        ]
        normed = norm(jnp.concatenate(levels, axis=0), ga_ref[...], D).astype(BF16)
        qkv[:, 0:D] = (dot(normed, wq[...]) * factor).astype(BF16)
        qkv[:, D : 3 * D] = dot(normed, wkv[...]).astype(BF16)

        def attend(window):
            row0 = window * WINDOW
            units = [(half, b) for half in range(2) for b in range(9)]
            scores, weights, heads = {}, {}, {}
            for half, b in units:
                col0 = half * 256
                keys = qkv[row0 : row0 + WINDOW, D + col0 : D + col0 + 256]
                query = qkv[row0 + 16 * b : row0 + 16 * b + 16, col0 : col0 + 256]
                spread = jnp.concatenate([query * m for m in head_mask], axis=0)
                scores[half, b] = lax.dot_general(
                    keys, spread, (((1,), (1,)), ((), ())), preferred_element_type=F32
                )
            for half, b in units:
                logits = scores[half, b] + bias[window, b]
                top = jnp.max(logits, axis=0, keepdims=True)
                raised = jnp.exp2(logits - top)
                total = jnp.sum(raised, axis=0, keepdims=True)
                weights[half, b] = (raised * (1.0 / total)).astype(BF16)
            for half, b in units:
                col0 = half * 256
                values = qkv[row0 : row0 + WINDOW, 2 * D + col0 : 2 * D + col0 + 256]
                heads[half, b] = lax.dot_general(
                    weights[half, b], values, (((0,), (0,)), ((), ())), preferred_element_type=F32
                )
            for half, b in units:
                picked = jnp.zeros((16, 256), F32)
                for h in range(8):
                    picked = jnp.where(head_lane == h, heads[half, b][16 * h : 16 * h + 16], picked)
                at = row0 + 16 * b
                att[at : at + 16, half * 256 : half * 256 + 256] = picked.astype(BF16)

        if g == 0:
            for window in range(2):
                attend(window)
            loads[7].wait()
            back0[...] = dot(fromwin0[...], att[...]).astype(BF16)
            rows = pl.ds(144, 144)
            second.append([remote(4, back0.at[rows], home0.at[rows], upper[0])])
            second[0][0].start()
        else:
            loads[8].wait()
            second.append([])
            for window in range(2):
                attend(window)
                moved = dot(fromwin1[...], att[window * WINDOW : window * WINDOW + WINDOW, :])
                back1[window] = moved.reshape(20, 8, D).astype(BF16)
                for i in range(3):
                    part = (window, pl.ds(5 * i + 5, 5))
                    copy = remote(5 + 3 * window + i, back1.at[part], home1.at[part], upper[i])
                    copy.start()
                    second[1].append(copy)

    for i in (9, 10, 11, 12, 13, 18, 19):
        loads[i].wait()
    for g in range(2):
        for copy in second[g]:
            copy.wait_recv()
        if g == 0:
            staged = jnp.concatenate([back0[0:144], home0[144:]], axis=0)
        else:
            parts = [r for w in range(2) for r in (back1[w, 0:5], home1[w, 5:20])]
            staged = jnp.concatenate([r.astype(F32).reshape(-1, D) for r in parts], axis=0).astype(BF16)
        attended = dot(tofinal[g][...], staged).astype(BF16)
        after = (resid[g] + dot(attended, wo[...])).astype(BF16)
        after_wide = after.astype(F32)
        normed = norm(after_wide, gm_ref[...], D).astype(BF16)
        total = after_wide
        for c in range(2):
            cols = slice(c * 1024, c * 1024 + 1024)
            up = dot(normed, wup[:, cols])
            hidden = (0.5 * up * (1.0 + lax.erf(up * (2.0 ** -0.5)))).astype(BF16)
            total = total + dot(hidden, wdn[cols, :])
        done = total.astype(BF16).astype(F32)
        for pos in range(4):
            for jslot, j in enumerate(MERGE_COLS[g][pos // 2]):
                at = pos * 72 + jslot * 24
                joined[24 * j : 24 * j + 24, D * pos : D * pos + D] = done[at : at + 24]

    loads[14].wait()
    merged = dot(norm(joined[...], gg_ref[...], 4 * D).astype(BF16), wm[...])
    for j in range(6):
        tiles = merged[24 * j : 24 * j + 24].reshape(6, 4, MERGED).astype(BF16)
        for i in range(6):
            out_ref[i, j] = tiles[i]
    for copy in first[1:] + second[0] + second[1]:
        copy.wait_send()


def on_device(
    lat_count, lon_count, patches, w_query, w_keyval, w_out, w_up, w_down, w_merge,
    gain_attn, gain_mlp, gain_merge, lat_valid, region_ids,
):
    perms = [jnp.asarray(m) for m in permutations()]
    hbm = pl.BlockSpec(memory_space=pl.ANY)
    vmem = pl.BlockSpec(memory_space=pltpu.VMEM)
    grid = patches.transpose(1, 2, 0, 3)
    weights = (w_query, w_keyval, w_out, w_up, w_down, w_merge)
    held = [pltpu.VMEM(v.shape, v.dtype) for v in (grid,) + weights + tuple(perms)]
    merged = pl.pallas_call(
        functools.partial(kernel, lat_count, lon_count),
        out_shape=pltpu.VMEM((6, 6, 4, MERGED), BF16),
        in_specs=[hbm] * 18,
        out_specs=vmem,
        scratch_shapes=held
        + [
            pltpu.VMEM((1, D), F32),
            pltpu.VMEM((1, D), F32),
            pltpu.VMEM((1, 4 * D), F32),
            pltpu.SMEM(lat_valid.shape, jnp.int32),
            pltpu.SMEM(region_ids.shape, jnp.int32),
            pltpu.VMEM((12, 6, 4, D), BF16),
            pltpu.VMEM((12, 6, 4, D), BF16),
            pltpu.VMEM((BACK_ROWS[0], D), BF16),
            pltpu.VMEM((2, 20, 8, D), BF16),
            pltpu.VMEM((BACK_ROWS[0], D), BF16),
            pltpu.VMEM((2, 20, 8, D), BF16),
            pltpu.VMEM((4, CELLS, 128), F32),
            pltpu.VMEM((CELLS, 3 * D), BF16),
            pltpu.VMEM((CELLS, D), BF16),
            pltpu.VMEM((2, 9, WINDOW, 128), F32),
            pltpu.VMEM((2, CELLS, D), F32),
            pltpu.VMEM((144, 4 * D), F32),
            pltpu.SemaphoreType.DMA((20,)),
            pltpu.SemaphoreType.DMA((11,)),
            pltpu.SemaphoreType.DMA((11,)),
        ],
        compiler_params=pltpu.CompilerParams(
            collective_id=0, has_side_effects=True, vmem_limit_bytes=56 * 1024 * 1024
        ),
        cost_estimate=pl.CostEstimate(
            flops=6_000_000_000, bytes_accessed=12_000_000, transcendentals=3_000_000
        ),
    )(
        grid, *weights, *perms,
        gain_attn.reshape(1, -1), gain_mlp.reshape(1, -1), gain_merge.reshape(1, -1),
        lat_valid, region_ids,
    )
    return merged.transpose(2, 0, 1, 3)


def solution(mesh):
    placed = (P(None, "lat", "lon", None),) + (P(),) * 11
    return jax.shard_map(
        functools.partial(on_device, mesh.shape["lat"], mesh.shape["lon"]),
        mesh=mesh,
        in_specs=placed,
        out_specs=P(None, "lat", "lon", None),
        check_vma=False,
    )
```

```python
import functools
import math

import jax
import jax.numpy as jnp
import numpy as np
from jax import lax
from jax.experimental import pallas as pl
from jax.experimental.pallas import tpu as pltpu
from jax.sharding import PartitionSpec as P

HEADS = 16
D = 512
FFN = 2048
MERGED = 1024
WIN_LAT = 12
SHIFT_LAT = 6
EPSILON = 1e-05
MESH = pl.DeviceIdType.MESH
F32 = jnp.float32
BF16 = jnp.bfloat16

CELLS = 288
WINDOW = 144
LEVEL_SLOTS = (1, 2, 3, 0)
MERGE_COLS = (((2, 3, 4), (1, 2, 3)), ((5, 0, 1), (4, 5, 0)))


def permutations():
    result = []
    for g in range(2):
        from_win = np.zeros((CELLS, CELLS), np.float32)
        to_final = np.zeros((CELLS, CELLS), np.float32)
        flat_final = np.zeros((CELLS, 576), np.float32)
        for slot, lev in enumerate(LEVEL_SLOTS):
            for wr in range(12):
                for wc in range(6):
                    win = slot * 72 + wr * 6 + wc
                    if g == 0:
                        seg = (wr // 6) * 144 + slot * 36 + (wr % 6) * 6 + wc
                    else:
                        part = wr // 6 + 2 * (wc // 3)
                        seg = part * 72 + slot * 18 + (wr % 6) * 3 + wc % 3
                    row, col = (wr + 6) % 12, (wc + 3 + 6 * g) % 12
                    pos = row % 2 + 2 * (col % 2)
                    jslot = MERGE_COLS[g][col % 2].index(col // 2)
                    final = pos * 72 + jslot * 24 + (row // 2) * 4 + lev
                    from_win[seg, win] = 1
                    to_final[final, seg] = 1
                    flat_final[final, (row * 12 + col) * 4 + lev] = 1
        result += [from_win, to_final, flat_final]
    return [m.astype(jnp.bfloat16) for m in result]


def norm(wide, gain, width):
    average = jnp.sum(wide, axis=-1, keepdims=True) * (1.0 / width)
    centred = wide - average
    variance = jnp.sum(centred * centred, axis=-1, keepdims=True) * (1.0 / width)
    return centred * lax.rsqrt(variance + EPSILON) * gain


def dot(a, b):
    return jnp.dot(a, b, preferred_element_type=F32)


def kernel(
    lat_count,
    lon_count,
    x_hbm, wq_hbm, wkv_hbm, wo_hbm, wup_hbm, wdn_hbm, wm_hbm,
    fromwin0_hbm, tofinal0_hbm, flat0_hbm, fromwin1_hbm, tofinal1_hbm, flat1_hbm,
    ga_hbm, gm_hbm, gg_hbm, valid_hbm, region_hbm,
    out_ref,
    x_v, wq, wkv, wo, wup, wdn, wm,
    fromwin0, tofinal0, flat0, fromwin1, tofinal1, flat1,
    ga_ref, gm_ref, gg_ref, valid_ref, region_ref,
    cells0, cells1, back0, back1, home0, home1, wide, qkv, att, bias, resid, joined,
    local_sem, send_sem, recv_sem,
):
    a, o = lax.axis_index("lat"), lax.axis_index("lon")
    lat_dn = lax.rem(a + lat_count - 1, lat_count)
    lat_up = lax.rem(a + 1, lat_count)
    lon_dn = lax.rem(o + lon_count - 1, lon_count)
    lon_up = lax.rem(o + 1, lon_count)
    lower = ((lat_dn, o), (a, lon_dn), (lat_dn, lon_dn))
    upper = ((lat_up, o), (a, lon_up), (lat_up, lon_up))
    cells, tofinal, flat = (cells0, cells1), (tofinal0, tofinal1), (flat0, flat1)

    barrier = pltpu.get_barrier_semaphore()
    for device in upper:
        pl.semaphore_signal(barrier, inc=1, device_id=device, device_id_type=MESH)

    pairs = (
        (x_hbm.at[pl.ds(6, 6), pl.ds(3, 6)], cells0.at[pl.ds(0, 6)]),
        (x_hbm.at[pl.ds(6, 6), pl.ds(9, 3)], cells1.at[pl.ds(0, 6), pl.ds(0, 3)]),
        (x_hbm, x_v), (wq_hbm, wq), (wkv_hbm, wkv), (flat0_hbm, flat0), (flat1_hbm, flat1),
        (fromwin0_hbm, fromwin0), (fromwin1_hbm, fromwin1),
        (tofinal0_hbm, tofinal0), (tofinal1_hbm, tofinal1),
        (wo_hbm, wo), (wup_hbm, wup), (wdn_hbm, wdn), (wm_hbm, wm),
        (region_hbm, region_ref), (valid_hbm, valid_ref),
        (ga_hbm, ga_ref), (gm_hbm, gm_ref), (gg_hbm, gg_ref),
    )
    loads = [pltpu.make_async_copy(s, d, local_sem.at[i]) for i, (s, d) in enumerate(pairs)]

    def remote(slot, source, target, device):
        return pltpu.make_async_remote_copy(
            src_ref=source, dst_ref=target, send_sem=send_sem.at[slot], recv_sem=recv_sem.at[slot],
            device_id=device, device_id_type=MESH,
        )

    first = [
        remote(0, x_hbm.at[pl.ds(0, 6), pl.ds(3, 6)], cells0.at[pl.ds(6, 6)], lower[0]),
        remote(1, x_hbm.at[pl.ds(0, 6), pl.ds(0, 3)], cells1.at[pl.ds(6, 6), pl.ds(3, 3)], lower[2]),
        remote(2, x_hbm.at[pl.ds(6, 6), pl.ds(0, 3)], cells1.at[pl.ds(0, 6), pl.ds(3, 3)], lower[1]),
        remote(3, x_hbm.at[pl.ds(0, 6), pl.ds(9, 3)], cells1.at[pl.ds(6, 6), pl.ds(0, 3)], lower[0]),
    ]
    for load in loads[15:17] + loads[:3]:
        load.start()
    pl.semaphore_wait(barrier, 3)
    for copy in first:
        copy.start()
    for load in loads[17:] + loads[3:15]:
        load.start()

    key_row = lax.broadcasted_iota(jnp.int32, (WINDOW, 128), 0)
    key_lev = (key_row >= 72).astype(jnp.int32)
    key_lat = ((key_row - 72 * key_lev) * 683) >> 12
    start = a * WIN_LAT + SHIFT_LAT
    loads[15].wait()
    loads[16].wait()
    row_ids = [lax.rem(start + r, lat_count * WIN_LAT) for r in range(WIN_LAT)]
    tags = [region_ref[i] for i in row_ids]
    valid = [valid_ref[i] for i in row_ids]
    key_tag = jnp.zeros((WINDOW, 128), jnp.int32)
    key_valid = jnp.zeros((WINDOW, 128), jnp.int32)
    for r in range(WIN_LAT):
        key_tag = jnp.where(key_lat == r, tags[r], key_tag)
        key_valid = jnp.where(key_lat == r, valid[r], key_valid)
    lane = lax.broadcasted_iota(jnp.int32, (1, 128), 1) & 15
    for b in range(9):
        query = lane + 16 * b
        query_lev = (query >= 72).astype(jnp.int32)
        query_lat = ((query - 72 * query_lev) * 683) >> 12
        query_tag = jnp.zeros((1, 128), jnp.int32)
        for r in range(WIN_LAT):
            query_tag = jnp.where(query_lat == r, tags[r], query_tag)
        usable = (key_tag == query_tag) & ((key_valid == 1) | (key_row == query))
        bias[0, b] = jnp.where(usable, 0.0, -jnp.inf)
        bias[1, b] = jnp.where(usable & (key_lev == query_lev), 0.0, -jnp.inf)

    first[0].wait_send()

    for i in (2, 5, 6, 17):
        loads[i].wait()
    mine = jnp.concatenate([x_v[r].astype(F32).reshape(48, D) for r in range(12)], axis=0).astype(BF16)
    for g in range(2):
        resid[g] = dot(flat[g][...], mine)

    head_lane = lax.broadcasted_iota(jnp.int32, (16, 256), 1) >> 5
    head_mask = [(head_lane == h).astype(F32).astype(BF16) for h in range(8)]
    factor = math.log2(math.e) / math.sqrt(D // HEADS)

    second = []
    for g in range(2):
        loads[g].wait()
        for copy in (first[:1], first[1:])[g]:
            copy.wait_recv()
        if g == 0:
            loads[3].wait()
            loads[4].wait()
        for row in range(12):
            flat_row = cells[g][row].astype(F32).reshape(24, D)
            for c in range(4):
                wide[c, 24 * row : 24 * row + 24, :] = flat_row[:, 128 * c : 128 * c + 128]
        levels = [
            jnp.concatenate([wide[c, pl.ds(lev, 72, stride=4), :] for c in range(4)], axis=1)
            for lev in LEVEL_SLOTS
        ]
        normed = norm(jnp.concatenate(levels, axis=0), ga_ref[...], D).astype(BF16)
        qkv[:, 0:D] = dot(normed, wq[...]).astype(BF16)
        qkv[:, D : 3 * D] = dot(normed, wkv[...]).astype(BF16)

        def attend(half):
            col0 = half * 256
            units = [(window, b) for window in range(2) for b in range(9)]
            scores, weights, heads = {}, {}, {}
            for window, b in units:
                row0 = window * WINDOW
                keys = qkv[row0 : row0 + WINDOW, D + col0 : D + col0 + 256]
                query = qkv[row0 + 16 * b : row0 + 16 * b + 16, col0 : col0 + 256]
                spread = jnp.concatenate([query * m for m in head_mask], axis=0)
                scores[window, b] = lax.dot_general(
                    keys, spread, (((1,), (1,)), ((), ())), preferred_element_type=F32
                )
            for window, b in units:
                logits = scores[window, b] * factor + bias[window, b]
                top = jnp.max(logits, axis=0, keepdims=True)
                raised = jnp.exp2(logits - top)
                total = jnp.sum(raised, axis=0, keepdims=True)
                weights[window, b] = (raised * (1.0 / total)).astype(BF16)
            for window, b in units:
                row0 = window * WINDOW
                values = qkv[row0 : row0 + WINDOW, 2 * D + col0 : 2 * D + col0 + 256]
                heads[window, b] = lax.dot_general(
                    weights[window, b], values, (((0,), (0,)), ((), ())), preferred_element_type=F32
                )
            for window, b in units:
                picked = jnp.zeros((16, 256), F32)
                for h in range(8):
                    picked = jnp.where(head_lane == h, heads[window, b][16 * h : 16 * h + 16], picked)
                at = window * WINDOW + 16 * b
                att[at : at + 16, col0 : col0 + 256] = picked.astype(BF16)

        loads[7 + g].wait()
        second.append([])
        if g == 0:
            for half in range(2):
                attend(half)
            back0[...] = dot(fromwin0[...], att[...]).astype(BF16)
            part = pl.ds(144, 144)
            second[0].append(remote(4, back0.at[part], home0.at[part], upper[0]))
            second[0][0].start()
        else:
            for half in range(2):
                attend(half)
                moved = dot(fromwin1[...], att[:, 256 * half : 256 * half + 256])
                back1[half] = moved.reshape(36, 8, 256).astype(BF16)
                for i in range(3):
                    part = (half, pl.ds(9 * i + 9, 9))
                    copy = remote(5 + 3 * half + i, back1.at[part], home1.at[part], upper[i])
                    copy.start()
                    second[1].append(copy)

    for i in (9, 10, 11, 12, 13, 18, 19):
        loads[i].wait()
    for g in range(2):
        for copy in second[g]:
            copy.wait_recv()
        if g == 0:
            staged = jnp.concatenate([back0[0:144], home0[144:288]], axis=0)
        else:
            parts = [jnp.concatenate([back1[h, 0:9], home1[h, 9:36]], axis=0) for h in range(2)]
            parts = [r.astype(F32).reshape(CELLS, 256) for r in parts]
            staged = jnp.concatenate(parts, axis=1).astype(BF16)
        attended = dot(tofinal[g][...], staged).astype(BF16)
        after = (resid[g] + dot(attended, wo[...])).astype(BF16)
        after_wide = after.astype(F32)
        normed = norm(after_wide, gm_ref[...], D).astype(BF16)
        total = after_wide
        for c in range(2):
            cols = slice(c * 1024, c * 1024 + 1024)
            up = dot(normed, wup[:, cols])
            hidden = (0.5 * up * (1.0 + lax.erf(up * (2.0 ** -0.5)))).astype(BF16)
            total = total + dot(hidden, wdn[cols, :])
        done = total.astype(BF16).astype(F32)
        for pos in range(4):
            for jslot, j in enumerate(MERGE_COLS[g][pos // 2]):
                at = pos * 72 + jslot * 24
                joined[24 * j : 24 * j + 24, D * pos : D * pos + D] = done[at : at + 24]

    loads[14].wait()
    merged = dot(norm(joined[...], gg_ref[...], 4 * D).astype(BF16), wm[...])
    for j in range(6):
        tiles = merged[24 * j : 24 * j + 24].reshape(6, 4, MERGED).astype(BF16)
        for i in range(6):
            out_ref[i, j] = tiles[i]
    for copy in first[1:] + second[0] + second[1]:
        copy.wait_send()


def on_device(
    lat_count, lon_count, patches, w_query, w_keyval, w_out, w_up, w_down, w_merge,
    gain_attn, gain_mlp, gain_merge, lat_valid, region_ids,
):
    perms = [jnp.asarray(m) for m in permutations()]
    hbm = pl.BlockSpec(memory_space=pl.ANY)
    vmem = pl.BlockSpec(memory_space=pltpu.VMEM)
    grid = patches.transpose(1, 2, 0, 3)
    weights = (w_query, w_keyval, w_out, w_up, w_down, w_merge)
    held = [pltpu.VMEM(v.shape, v.dtype) for v in (grid,) + weights + tuple(perms)]
    merged = pl.pallas_call(
        functools.partial(kernel, lat_count, lon_count),
        out_shape=pltpu.VMEM((6, 6, 4, MERGED), BF16),
        in_specs=[hbm] * 18,
        out_specs=vmem,
        scratch_shapes=held
        + [
            pltpu.VMEM((1, D), F32),
            pltpu.VMEM((1, D), F32),
            pltpu.VMEM((1, 4 * D), F32),
            pltpu.SMEM(lat_valid.shape, jnp.int32),
            pltpu.SMEM(region_ids.shape, jnp.int32),
            pltpu.VMEM((12, 6, 4, D), BF16),
            pltpu.VMEM((12, 6, 4, D), BF16),
            pltpu.VMEM((CELLS, D), BF16),
            pltpu.VMEM((2, 36, 8, 256), BF16),
            pltpu.VMEM((CELLS, D), BF16),
            pltpu.VMEM((2, 36, 8, 256), BF16),
            pltpu.VMEM((4, CELLS, 128), F32),
            pltpu.VMEM((CELLS, 3 * D), BF16),
            pltpu.VMEM((CELLS, D), BF16),
            pltpu.VMEM((2, 9, WINDOW, 128), F32),
            pltpu.VMEM((2, CELLS, D), F32),
            pltpu.VMEM((144, 4 * D), F32),
            pltpu.SemaphoreType.DMA((20,)),
            pltpu.SemaphoreType.DMA((11,)),
            pltpu.SemaphoreType.DMA((11,)),
        ],
        compiler_params=pltpu.CompilerParams(
            collective_id=0, has_side_effects=True, vmem_limit_bytes=56 * 1024 * 1024
        ),
        cost_estimate=pl.CostEstimate(
            flops=6_000_000_000, bytes_accessed=12_000_000, transcendentals=3_000_000
        ),
    )(
        grid, *weights, *perms,
        gain_attn.reshape(1, -1), gain_mlp.reshape(1, -1), gain_merge.reshape(1, -1),
        lat_valid, region_ids,
    )
    return merged.transpose(2, 0, 1, 3)


def solution(mesh):
    placed = (P(None, "lat", "lon", None),) + (P(),) * 11
    return jax.shard_map(
        functools.partial(on_device, mesh.shape["lat"], mesh.shape["lon"]),
        mesh=mesh,
        in_specs=placed,
        out_specs=P(None, "lat", "lon", None),
        check_vma=False,
    )
```

```python
import functools
import math

import jax
import jax.numpy as jnp
import numpy as np
from jax import lax
from jax.experimental import pallas as pl
from jax.experimental.pallas import tpu as pltpu
from jax.sharding import PartitionSpec as P

HEADS = 16
D = 512
FFN = 2048
MERGED = 1024
WIN_LAT = 12
SHIFT_LAT = 6
EPSILON = 1e-05
MESH = pl.DeviceIdType.MESH
F32 = jnp.float32
BF16 = jnp.bfloat16

CELLS = 288
WINDOW = 144
LEVEL_SLOTS = (1, 2, 3, 0)
MERGE_COLS = (((2, 3, 4), (1, 2, 3)), ((5, 0, 1), (4, 5, 0)))


def permutations():
    result = []
    for g in range(2):
        from_win = np.zeros((CELLS, CELLS), np.float32)
        to_final = np.zeros((CELLS, CELLS), np.float32)
        flat_final = np.zeros((CELLS, 576), np.float32)
        for slot, lev in enumerate(LEVEL_SLOTS):
            for wr in range(12):
                for wc in range(6):
                    win = slot * 72 + wr * 6 + wc
                    if g == 0:
                        seg = (wr // 6) * 144 + slot * 36 + (wr % 6) * 6 + wc
                    else:
                        part = wr // 6 + 2 * (wc // 3)
                        seg = part * 72 + slot * 18 + (wr % 6) * 3 + wc % 3
                    row, col = (wr + 6) % 12, (wc + 3 + 6 * g) % 12
                    pos = row % 2 + 2 * (col % 2)
                    jslot = MERGE_COLS[g][col % 2].index(col // 2)
                    final = pos * 72 + jslot * 24 + (row // 2) * 4 + lev
                    from_win[seg, win] = 1
                    to_final[final, seg] = 1
                    flat_final[final, (row * 12 + col) * 4 + lev] = 1
        result += [from_win, to_final, flat_final]
    return [m.astype(jnp.bfloat16) for m in result]


def norm(wide, gain, width):
    average = jnp.sum(wide, axis=-1, keepdims=True) * (1.0 / width)
    centred = wide - average
    variance = jnp.sum(centred * centred, axis=-1, keepdims=True) * (1.0 / width)
    return centred * lax.rsqrt(variance + EPSILON) * gain


def dot(a, b):
    return jnp.dot(a, b, preferred_element_type=F32)


def kernel(
    lat_count,
    lon_count,
    x_hbm, wq_hbm, wkv_hbm, wo_hbm, wup_hbm, wdn_hbm, wm_hbm,
    fromwin0_hbm, tofinal0_hbm, flat0_hbm, fromwin1_hbm, tofinal1_hbm, flat1_hbm,
    ga_hbm, gm_hbm, gg_hbm, valid_hbm, region_hbm,
    out_ref,
    x_v, wq, wkv, wo, wup, wdn, wm,
    fromwin0, tofinal0, flat0, fromwin1, tofinal1, flat1,
    ga_ref, gm_ref, gg_ref, valid_ref, region_ref,
    cells0, cells1, back0, back1, home0, home1, wide, qkv, att, bias, resid, joined,
    local_sem, send_sem, recv_sem,
):
    a, o = lax.axis_index("lat"), lax.axis_index("lon")
    lat_dn = lax.rem(a + lat_count - 1, lat_count)
    lat_up = lax.rem(a + 1, lat_count)
    lon_dn = lax.rem(o + lon_count - 1, lon_count)
    lon_up = lax.rem(o + 1, lon_count)
    lower = ((lat_dn, o), (a, lon_dn), (lat_dn, lon_dn))
    upper = ((lat_up, o), (a, lon_up), (lat_up, lon_up))
    cells, tofinal, flat = (cells0, cells1), (tofinal0, tofinal1), (flat0, flat1)

    barrier = pltpu.get_barrier_semaphore()
    for device in upper:
        pl.semaphore_signal(barrier, inc=1, device_id=device, device_id_type=MESH)

    pairs = (
        (x_hbm.at[pl.ds(6, 6), pl.ds(3, 6)], cells0.at[pl.ds(0, 6)]),
        (x_hbm.at[pl.ds(6, 6), pl.ds(9, 3)], cells1.at[pl.ds(0, 6), pl.ds(0, 3)]),
        (x_hbm, x_v), (wq_hbm, wq), (wkv_hbm, wkv), (flat0_hbm, flat0), (flat1_hbm, flat1),
        (fromwin0_hbm, fromwin0), (fromwin1_hbm, fromwin1),
        (tofinal0_hbm, tofinal0), (tofinal1_hbm, tofinal1),
        (wo_hbm, wo), (wup_hbm, wup), (wdn_hbm, wdn), (wm_hbm, wm),
        (region_hbm, region_ref), (valid_hbm, valid_ref),
        (ga_hbm, ga_ref), (gm_hbm, gm_ref), (gg_hbm, gg_ref),
    )
    loads = [pltpu.make_async_copy(s, d, local_sem.at[i]) for i, (s, d) in enumerate(pairs)]

    def remote(slot, source, target, device):
        return pltpu.make_async_remote_copy(
            src_ref=source, dst_ref=target, send_sem=send_sem.at[slot], recv_sem=recv_sem.at[slot],
            device_id=device, device_id_type=MESH,
        )

    first = [
        remote(0, x_hbm.at[pl.ds(0, 6), pl.ds(3, 6)], cells0.at[pl.ds(6, 6)], lower[0]),
        remote(1, x_hbm.at[pl.ds(0, 6), pl.ds(0, 3)], cells1.at[pl.ds(6, 6), pl.ds(3, 3)], lower[2]),
        remote(2, x_hbm.at[pl.ds(6, 6), pl.ds(0, 3)], cells1.at[pl.ds(0, 6), pl.ds(3, 3)], lower[1]),
        remote(3, x_hbm.at[pl.ds(0, 6), pl.ds(9, 3)], cells1.at[pl.ds(6, 6), pl.ds(0, 3)], lower[0]),
    ]
    for load in loads[15:17] + loads[:3]:
        load.start()
    pl.semaphore_wait(barrier, 3)
    for copy in first:
        copy.start()
    for load in loads[17:] + loads[3:15]:
        load.start()

    key_row = lax.broadcasted_iota(jnp.int32, (WINDOW, 128), 0)
    key_lev = (key_row >= 72).astype(jnp.int32)
    key_lat = ((key_row - 72 * key_lev) * 683) >> 12
    start = a * WIN_LAT + SHIFT_LAT
    loads[15].wait()
    loads[16].wait()
    row_ids = [lax.rem(start + r, lat_count * WIN_LAT) for r in range(WIN_LAT)]
    tags = [region_ref[i] for i in row_ids]
    valid = [valid_ref[i] for i in row_ids]
    key_tag = jnp.zeros((WINDOW, 128), jnp.int32)
    key_valid = jnp.zeros((WINDOW, 128), jnp.int32)
    for r in range(WIN_LAT):
        key_tag = jnp.where(key_lat == r, tags[r], key_tag)
        key_valid = jnp.where(key_lat == r, valid[r], key_valid)
    lane = lax.broadcasted_iota(jnp.int32, (1, 128), 1) & 15
    for b in range(9):
        query = lane + 16 * b
        query_lev = (query >= 72).astype(jnp.int32)
        query_lat = ((query - 72 * query_lev) * 683) >> 12
        query_tag = jnp.zeros((1, 128), jnp.int32)
        for r in range(WIN_LAT):
            query_tag = jnp.where(query_lat == r, tags[r], query_tag)
        usable = (key_tag == query_tag) & ((key_valid == 1) | (key_row == query))
        bias[0, b] = jnp.where(usable, 0.0, -jnp.inf)
        bias[1, b] = jnp.where(usable & (key_lev == query_lev), 0.0, -jnp.inf)

    first[0].wait_send()

    for i in (2, 5, 6, 17):
        loads[i].wait()
    mine = jnp.concatenate([x_v[r].astype(F32).reshape(48, D) for r in range(12)], axis=0).astype(BF16)
    for g in range(2):
        resid[g] = dot(flat[g][...], mine)

    head_lane = lax.broadcasted_iota(jnp.int32, (16, 256), 1) >> 5
    head_mask = [(head_lane == h).astype(F32).astype(BF16) for h in range(8)]
    factor = math.log2(math.e) / math.sqrt(D // HEADS)

    second = []
    for g in range(2):
        loads[g].wait()
        for copy in (first[:1], first[1:])[g]:
            copy.wait_recv()
        if g == 0:
            loads[3].wait()
            loads[4].wait()
        for row in range(12):
            flat_row = cells[g][row].astype(F32).reshape(24, D)
            for c in range(4):
                wide[c, 24 * row : 24 * row + 24, :] = flat_row[:, 128 * c : 128 * c + 128]
        levels = [
            jnp.concatenate([wide[c, pl.ds(lev, 72, stride=4), :] for c in range(4)], axis=1)
            for lev in LEVEL_SLOTS
        ]
        normed = norm(jnp.concatenate(levels, axis=0), ga_ref[...], D).astype(BF16)
        qkv[:, 0:D] = dot(normed, wq[...]).astype(BF16)
        qkv[:, D : 3 * D] = dot(normed, wkv[...]).astype(BF16)

        def attend(half):
            col0 = half * 256
            units = [(window, b) for window in range(2) for b in range(9)]
            scores, weights, heads = {}, {}, {}
            for window, b in units:
                row0 = window * WINDOW
                keys = qkv[row0 : row0 + WINDOW, D + col0 : D + col0 + 256]
                query = qkv[row0 + 16 * b : row0 + 16 * b + 16, col0 : col0 + 256]
                spread = jnp.concatenate([query * m for m in head_mask], axis=0)
                scores[window, b] = lax.dot_general(
                    keys, spread, (((1,), (1,)), ((), ())), preferred_element_type=F32
                )
            for window, b in units:
                logits = scores[window, b] * factor + bias[window, b]
                top = jnp.max(logits, axis=0, keepdims=True)
                raised = jnp.exp2(logits - top)
                total = jnp.sum(raised, axis=0, keepdims=True)
                weights[window, b] = (raised * (1.0 / total)).astype(BF16)
            for window, b in units:
                row0 = window * WINDOW
                values = qkv[row0 : row0 + WINDOW, 2 * D + col0 : 2 * D + col0 + 256]
                heads[window, b] = lax.dot_general(
                    weights[window, b], values, (((0,), (0,)), ((), ())), preferred_element_type=F32
                )
            for window, b in units:
                picked = jnp.zeros((16, 256), F32)
                for h in range(8):
                    picked = jnp.where(head_lane == h, heads[window, b][16 * h : 16 * h + 16], picked)
                at = window * WINDOW + 16 * b
                att[at : at + 16, col0 : col0 + 256] = picked.astype(BF16)

        loads[7 + g].wait()
        second.append([])
        if g == 0:
            for half in range(2):
                attend(half)
            back0[...] = dot(fromwin0[...], att[...]).astype(BF16)
            part = pl.ds(144, 144)
            second[0].append(remote(4, back0.at[part], home0.at[part], upper[0]))
            second[0][0].start()
        else:
            for half in range(2):
                attend(half)
                moved = dot(fromwin1[...], att[:, 256 * half : 256 * half + 256])
                back1[half] = moved.reshape(36, 8, 256).astype(BF16)
                for i in (2, 1, 0):
                    part = (half, pl.ds(9 * i + 9, 9))
                    copy = remote(5 + 3 * half + i, back1.at[part], home1.at[part], upper[i])
                    copy.start()
                    second[1].append(copy)

    for i in (9, 10, 11, 12, 13, 14, 18, 19):
        loads[i].wait()

    for g in range(2):
        if g == 0:
            second[0][0].wait_recv()
            staged = jnp.concatenate([back0[0:144], home0[144:288]], axis=0)
            attended = dot(tofinal[0][...], staged).astype(BF16)
            after = (resid[0] + dot(attended, wo[...])).astype(BF16)
        else:
            after = resid[1]
            for half in range(2):
                for copy in second[1][3 * half : 3 * half + 3]:
                    copy.wait_recv()
                tiles = jnp.concatenate([back1[half, 0:9], home1[half, 9:36]], axis=0)
                staged = tiles.astype(F32).reshape(CELLS, 256).astype(BF16)
                attended = dot(tofinal[1][...], staged).astype(BF16)
                after = after + dot(attended, wo[256 * half : 256 * half + 256, :])
            after = after.astype(BF16)
        after_wide = after.astype(F32)
        normed = norm(after_wide, gm_ref[...], D).astype(BF16)
        total = after_wide
        for c in range(2):
            cols = slice(c * 1024, c * 1024 + 1024)
            up = dot(normed, wup[:, cols])
            hidden = (0.5 * up * (1.0 + lax.erf(up * (2.0 ** -0.5)))).astype(BF16)
            total = total + dot(hidden, wdn[cols, :])
        done = total.astype(BF16).astype(F32)
        for pos in range(4):
            for jslot, j in enumerate(MERGE_COLS[g][pos // 2]):
                at = pos * 72 + jslot * 24
                joined[24 * j : 24 * j + 24, D * pos : D * pos + D] = done[at : at + 24]
    merged = dot(norm(joined[...], gg_ref[...], 4 * D).astype(BF16), wm[...])
    for j in range(6):
        tiles = merged[24 * j : 24 * j + 24].reshape(6, 4, MERGED).astype(BF16)
        for i in range(6):
            out_ref[i, j] = tiles[i]

    for copy in first[1:] + second[0] + second[1]:
        copy.wait_send()


def on_device(
    lat_count, lon_count, patches, w_query, w_keyval, w_out, w_up, w_down, w_merge,
    gain_attn, gain_mlp, gain_merge, lat_valid, region_ids,
):
    perms = [jnp.asarray(m) for m in permutations()]
    hbm = pl.BlockSpec(memory_space=pl.ANY)
    vmem = pl.BlockSpec(memory_space=pltpu.VMEM)
    grid = patches.transpose(1, 2, 0, 3)
    weights = (w_query, w_keyval, w_out, w_up, w_down, w_merge)
    held = [pltpu.VMEM(v.shape, v.dtype) for v in (grid,) + weights + tuple(perms)]
    merged = pl.pallas_call(
        functools.partial(kernel, lat_count, lon_count),
        out_shape=pltpu.VMEM((6, 6, 4, MERGED), BF16),
        in_specs=[hbm] * 18,
        out_specs=vmem,
        scratch_shapes=held
        + [
            pltpu.VMEM((1, D), F32),
            pltpu.VMEM((1, D), F32),
            pltpu.VMEM((1, 4 * D), F32),
            pltpu.SMEM(lat_valid.shape, jnp.int32),
            pltpu.SMEM(region_ids.shape, jnp.int32),
            pltpu.VMEM((12, 6, 4, D), BF16),
            pltpu.VMEM((12, 6, 4, D), BF16),
            pltpu.VMEM((CELLS, D), BF16),
            pltpu.VMEM((2, 36, 8, 256), BF16),
            pltpu.VMEM((CELLS, D), BF16),
            pltpu.VMEM((2, 36, 8, 256), BF16),
            pltpu.VMEM((4, CELLS, 128), F32),
            pltpu.VMEM((CELLS, 3 * D), BF16),
            pltpu.VMEM((CELLS, D), BF16),
            pltpu.VMEM((2, 9, WINDOW, 128), F32),
            pltpu.VMEM((2, CELLS, D), F32),
            pltpu.VMEM((144, 4 * D), F32),
            pltpu.SemaphoreType.DMA((20,)),
            pltpu.SemaphoreType.DMA((11,)),
            pltpu.SemaphoreType.DMA((11,)),
        ],
        compiler_params=pltpu.CompilerParams(
            collective_id=0, has_side_effects=True, vmem_limit_bytes=56 * 1024 * 1024
        ),
        cost_estimate=pl.CostEstimate(
            flops=6_000_000_000, bytes_accessed=12_000_000, transcendentals=3_000_000
        ),
    )(
        grid, *weights, *perms,
        gain_attn.reshape(1, -1), gain_mlp.reshape(1, -1), gain_merge.reshape(1, -1),
        lat_valid, region_ids,
    )
    return merged.transpose(2, 0, 1, 3)


def solution(mesh):
    placed = (P(None, "lat", "lon", None),) + (P(),) * 11
    return jax.shard_map(
        functools.partial(on_device, mesh.shape["lat"], mesh.shape["lon"]),
        mesh=mesh,
        in_specs=placed,
        out_specs=P(None, "lat", "lon", None),
        check_vma=False,
    )
```

```python
import functools
import math

import jax
import jax.numpy as jnp
import numpy as np
from jax import lax
from jax.experimental import pallas as pl
from jax.experimental.pallas import tpu as pltpu
from jax.sharding import PartitionSpec as P

HEADS = 16
D = 512
FFN = 2048
MERGED = 1024
WIN_LAT = 12
SHIFT_LAT = 6
EPSILON = 1e-05
MESH = pl.DeviceIdType.MESH
F32 = jnp.float32
BF16 = jnp.bfloat16

CELLS = 288
WINDOW = 144
LEVEL_SLOTS = (1, 2, 3, 0)
MERGE_COLS = (((2, 3, 4), (1, 2, 3)), ((5, 0, 1), (4, 5, 0)))


def permutations():
    result = []
    for g in range(2):
        from_win = np.zeros((CELLS, CELLS), np.float32)
        to_final = np.zeros((CELLS, CELLS), np.float32)
        flat_final = np.zeros((CELLS, 576), np.float32)
        for slot, lev in enumerate(LEVEL_SLOTS):
            for wr in range(12):
                for wc in range(6):
                    win = slot * 72 + wr * 6 + wc
                    if g == 0:
                        seg = (wr // 6) * 144 + slot * 36 + (wr % 6) * 6 + wc
                    else:
                        part = wr // 6 + 2 * (wc // 3)
                        seg = part * 72 + slot * 18 + (wr % 6) * 3 + wc % 3
                    row, col = (wr + 6) % 12, (wc + 3 + 6 * g) % 12
                    pos = row % 2 + 2 * (col % 2)
                    jslot = MERGE_COLS[g][col % 2].index(col // 2)
                    final = pos * 72 + jslot * 24 + (row // 2) * 4 + lev
                    from_win[seg, win] = 1
                    to_final[final, seg] = 1
                    flat_final[final, (row * 12 + col) * 4 + lev] = 1
        result += [from_win, to_final, flat_final]
    return [m.astype(jnp.bfloat16) for m in result]


def norm(wide, gain, width):
    average = jnp.sum(wide, axis=-1, keepdims=True) * (1.0 / width)
    centred = wide - average
    variance = jnp.sum(centred * centred, axis=-1, keepdims=True) * (1.0 / width)
    return centred * lax.rsqrt(variance + EPSILON) * gain


def dot(a, b):
    return jnp.dot(a, b, preferred_element_type=F32)


def kernel(
    lat_count,
    lon_count,
    x_hbm, wq_hbm, wkv_hbm, wo_hbm, wup_hbm, wdn_hbm, wm_hbm,
    fromwin0_hbm, tofinal0_hbm, flat0_hbm, fromwin1_hbm, tofinal1_hbm, flat1_hbm,
    ga_hbm, gm_hbm, gg_hbm, valid_hbm, region_hbm,
    out_ref,
    x_v, wq, wkv, wo, wup, wdn, wm,
    fromwin0, tofinal0, flat0, fromwin1, tofinal1, flat1,
    ga_ref, gm_ref, gg_ref, valid_ref, region_ref,
    cells0, cells1, back0, back1, home0, home1, wide, qkv, att, bias, resid, joined,
    local_sem, send_sem, recv_sem,
):
    a, o = lax.axis_index("lat"), lax.axis_index("lon")
    lat_dn = lax.rem(a + lat_count - 1, lat_count)
    lat_up = lax.rem(a + 1, lat_count)
    lon_dn = lax.rem(o + lon_count - 1, lon_count)
    lon_up = lax.rem(o + 1, lon_count)
    lower = ((lat_dn, o), (a, lon_dn), (lat_dn, lon_dn))
    upper = ((lat_up, o), (a, lon_up), (lat_up, lon_up))
    cells, tofinal, flat = (cells0, cells1), (tofinal0, tofinal1), (flat0, flat1)

    barrier = pltpu.get_barrier_semaphore()
    for device in upper:
        pl.semaphore_signal(barrier, inc=1, device_id=device, device_id_type=MESH)

    pairs = (
        (x_hbm.at[pl.ds(6, 6), pl.ds(3, 6)], cells0.at[pl.ds(0, 6)]),
        (x_hbm.at[pl.ds(6, 6), pl.ds(9, 3)], cells1.at[pl.ds(0, 6), pl.ds(0, 3)]),
        (x_hbm, x_v), (wq_hbm, wq), (wkv_hbm, wkv), (flat0_hbm, flat0), (flat1_hbm, flat1),
        (fromwin0_hbm, fromwin0), (fromwin1_hbm, fromwin1),
        (tofinal0_hbm, tofinal0), (tofinal1_hbm, tofinal1),
        (wo_hbm, wo), (wup_hbm, wup), (wdn_hbm, wdn), (wm_hbm, wm),
        (region_hbm, region_ref), (valid_hbm, valid_ref),
        (ga_hbm, ga_ref), (gm_hbm, gm_ref), (gg_hbm, gg_ref),
    )
    loads = [pltpu.make_async_copy(s, d, local_sem.at[i]) for i, (s, d) in enumerate(pairs)]

    def remote(slot, source, target, device):
        return pltpu.make_async_remote_copy(
            src_ref=source, dst_ref=target, send_sem=send_sem.at[slot], recv_sem=recv_sem.at[slot],
            device_id=device, device_id_type=MESH,
        )

    first = [
        remote(0, x_hbm.at[pl.ds(0, 6), pl.ds(3, 6)], cells0.at[pl.ds(6, 6)], lower[0]),
        remote(1, x_hbm.at[pl.ds(0, 6), pl.ds(0, 3)], cells1.at[pl.ds(6, 6), pl.ds(3, 3)], lower[2]),
        remote(2, x_hbm.at[pl.ds(6, 6), pl.ds(0, 3)], cells1.at[pl.ds(0, 6), pl.ds(3, 3)], lower[1]),
        remote(3, x_hbm.at[pl.ds(0, 6), pl.ds(9, 3)], cells1.at[pl.ds(6, 6), pl.ds(0, 3)], lower[0]),
    ]
    for load in loads[15:17] + loads[:3]:
        load.start()
    pl.semaphore_wait(barrier, 3)
    for copy in first:
        copy.start()
    for load in loads[17:] + loads[3:15]:
        load.start()

    key_row = lax.broadcasted_iota(jnp.int32, (WINDOW, 128), 0)
    key_lev = (key_row >= 72).astype(jnp.int32)
    key_lat = ((key_row - 72 * key_lev) * 683) >> 12
    start = a * WIN_LAT + SHIFT_LAT
    loads[15].wait()
    loads[16].wait()
    row_ids = [lax.rem(start + r, lat_count * WIN_LAT) for r in range(WIN_LAT)]
    tags = [region_ref[i] for i in row_ids]
    valid = [valid_ref[i] for i in row_ids]
    key_tag = jnp.zeros((WINDOW, 128), jnp.int32)
    key_valid = jnp.zeros((WINDOW, 128), jnp.int32)
    for r in range(WIN_LAT):
        key_tag = jnp.where(key_lat == r, tags[r], key_tag)
        key_valid = jnp.where(key_lat == r, valid[r], key_valid)
    lane = lax.broadcasted_iota(jnp.int32, (1, 128), 1) & 15
    for b in range(9):
        query = lane + 16 * b
        query_lev = (query >= 72).astype(jnp.int32)
        query_lat = ((query - 72 * query_lev) * 683) >> 12
        query_tag = jnp.zeros((1, 128), jnp.int32)
        for r in range(WIN_LAT):
            query_tag = jnp.where(query_lat == r, tags[r], query_tag)
        usable = (key_tag == query_tag) & ((key_valid == 1) | (key_row == query))
        bias[0, b] = jnp.where(usable, 0.0, -jnp.inf)
        bias[1, b] = jnp.where(usable & (key_lev == query_lev), 0.0, -jnp.inf)

    first[0].wait_send()

    for i in (2, 5, 6, 17):
        loads[i].wait()
    mine = jnp.concatenate([x_v[r].astype(F32).reshape(48, D) for r in range(12)], axis=0).astype(BF16)
    for g in range(2):
        resid[g] = dot(flat[g][...], mine)

    head_lane = lax.broadcasted_iota(jnp.int32, (16, 256), 1) >> 5
    head_mask = [(head_lane == h).astype(F32).astype(BF16) for h in range(8)]
    factor = math.log2(math.e) / math.sqrt(D // HEADS)

    second = []
    for g in range(2):
        loads[g].wait()
        for copy in (first[:1], first[1:])[g]:
            copy.wait_recv()
        if g == 0:
            loads[3].wait()
            loads[4].wait()
        for row in range(12):
            flat_row = cells[g][row].astype(F32).reshape(24, D)
            for c in range(4):
                wide[c, 24 * row : 24 * row + 24, :] = flat_row[:, 128 * c : 128 * c + 128]
        levels = [
            jnp.concatenate([wide[c, pl.ds(lev, 72, stride=4), :] for c in range(4)], axis=1)
            for lev in LEVEL_SLOTS
        ]
        normed = norm(jnp.concatenate(levels, axis=0), ga_ref[...], D).astype(BF16)
        qkv[:, 0:D] = dot(normed, wq[...]).astype(BF16)
        qkv[:, D : 3 * D] = dot(normed, wkv[...]).astype(BF16)

        def attend(half):
            col0 = half * 256
            units = [(window, b) for window in range(2) for b in range(9)]
            scores, weights, heads = {}, {}, {}
            for window, b in units:
                row0 = window * WINDOW
                keys = qkv[row0 : row0 + WINDOW, D + col0 : D + col0 + 256]
                query = qkv[row0 + 16 * b : row0 + 16 * b + 16, col0 : col0 + 256]
                spread = jnp.concatenate([query * m for m in head_mask], axis=0)
                scores[window, b] = lax.dot_general(
                    keys, spread, (((1,), (1,)), ((), ())), preferred_element_type=F32
                )
            for window, b in units:
                logits = scores[window, b] * factor + bias[window, b]
                top = jnp.max(logits, axis=0, keepdims=True)
                raised = jnp.exp2(logits - top)
                total = jnp.sum(raised, axis=0, keepdims=True)
                weights[window, b] = (raised * (1.0 / total)).astype(BF16)
            for window, b in units:
                row0 = window * WINDOW
                values = qkv[row0 : row0 + WINDOW, 2 * D + col0 : 2 * D + col0 + 256]
                heads[window, b] = lax.dot_general(
                    weights[window, b], values, (((0,), (0,)), ((), ())), preferred_element_type=F32
                )
            for window, b in units:
                picked = jnp.zeros((16, 256), F32)
                for h in range(8):
                    picked = jnp.where(head_lane == h, heads[window, b][16 * h : 16 * h + 16], picked)
                at = window * WINDOW + 16 * b
                att[at : at + 16, col0 : col0 + 256] = picked.astype(BF16)

        loads[7 + g].wait()
        second.append([])
        if g == 0:
            for half in range(2):
                attend(half)
                moved = dot(fromwin0[...], att[:, 256 * half : 256 * half + 256])
                back0[half] = moved.astype(BF16)
                part = (half, pl.ds(144, 144))
                second[0].append(remote((4, 11)[half], back0.at[part], home0.at[part], upper[0]))
                second[0][half].start()
        else:
            for half in range(2):
                attend(half)
                moved = dot(fromwin1[...], att[:, 256 * half : 256 * half + 256])
                back1[half] = moved.reshape(36, 8, 256).astype(BF16)
                for i in (2, 1, 0):
                    part = (half, pl.ds(9 * i + 9, 9))
                    copy = remote(5 + 3 * half + i, back1.at[part], home1.at[part], upper[i])
                    copy.start()
                    second[1].append(copy)

    for i in (9, 10, 11, 12, 13, 14, 18, 19):
        loads[i].wait()

    for g in range(2):
        if g == 0:
            for copy in second[0]:
                copy.wait_recv()
            parts = [jnp.concatenate([back0[h, 0:144], home0[h, 144:288]], axis=0) for h in range(2)]
            staged = jnp.concatenate(parts, axis=1)
            attended = dot(tofinal[0][...], staged).astype(BF16)
            after = (resid[0] + dot(attended, wo[...])).astype(BF16)
        else:
            after = resid[1]
            for half in range(2):
                for copy in second[1][3 * half : 3 * half + 3]:
                    copy.wait_recv()
                tiles = jnp.concatenate([back1[half, 0:9], home1[half, 9:36]], axis=0)
                staged = tiles.astype(F32).reshape(CELLS, 256).astype(BF16)
                attended = dot(tofinal[1][...], staged).astype(BF16)
                after = after + dot(attended, wo[256 * half : 256 * half + 256, :])
            after = after.astype(BF16)
        after_wide = after.astype(F32)
        normed = norm(after_wide, gm_ref[...], D).astype(BF16)
        total = after_wide
        for c in range(2):
            cols = slice(c * 1024, c * 1024 + 1024)
            up = dot(normed, wup[:, cols])
            hidden = (0.5 * up * (1.0 + lax.erf(up * (2.0 ** -0.5)))).astype(BF16)
            total = total + dot(hidden, wdn[cols, :])
        done = total.astype(BF16).astype(F32)
        for pos in range(4):
            for jslot, j in enumerate(MERGE_COLS[g][pos // 2]):
                at = pos * 72 + jslot * 24
                joined[24 * j : 24 * j + 24, D * pos : D * pos + D] = done[at : at + 24]
    merged = dot(norm(joined[...], gg_ref[...], 4 * D).astype(BF16), wm[...])
    for j in range(6):
        tiles = merged[24 * j : 24 * j + 24].reshape(6, 4, MERGED).astype(BF16)
        for i in range(6):
            out_ref[i, j] = tiles[i]

    for copy in first[1:] + second[0] + second[1]:
        copy.wait_send()


def on_device(
    lat_count, lon_count, patches, w_query, w_keyval, w_out, w_up, w_down, w_merge,
    gain_attn, gain_mlp, gain_merge, lat_valid, region_ids,
):
    perms = [jnp.asarray(m) for m in permutations()]
    hbm = pl.BlockSpec(memory_space=pl.ANY)
    vmem = pl.BlockSpec(memory_space=pltpu.VMEM)
    grid = patches.transpose(1, 2, 0, 3)
    weights = (w_query, w_keyval, w_out, w_up, w_down, w_merge)
    held = [pltpu.VMEM(v.shape, v.dtype) for v in (grid,) + weights + tuple(perms)]
    merged = pl.pallas_call(
        functools.partial(kernel, lat_count, lon_count),
        out_shape=pltpu.VMEM((6, 6, 4, MERGED), BF16),
        in_specs=[hbm] * 18,
        out_specs=vmem,
        scratch_shapes=held
        + [
            pltpu.VMEM((1, D), F32),
            pltpu.VMEM((1, D), F32),
            pltpu.VMEM((1, 4 * D), F32),
            pltpu.SMEM(lat_valid.shape, jnp.int32),
            pltpu.SMEM(region_ids.shape, jnp.int32),
            pltpu.VMEM((12, 6, 4, D), BF16),
            pltpu.VMEM((12, 6, 4, D), BF16),
            pltpu.VMEM((2, CELLS, 256), BF16),
            pltpu.VMEM((2, 36, 8, 256), BF16),
            pltpu.VMEM((2, CELLS, 256), BF16),
            pltpu.VMEM((2, 36, 8, 256), BF16),
            pltpu.VMEM((4, CELLS, 128), F32),
            pltpu.VMEM((CELLS, 3 * D), BF16),
            pltpu.VMEM((CELLS, D), BF16),
            pltpu.VMEM((2, 9, WINDOW, 128), F32),
            pltpu.VMEM((2, CELLS, D), F32),
            pltpu.VMEM((144, 4 * D), F32),
            pltpu.SemaphoreType.DMA((20,)),
            pltpu.SemaphoreType.DMA((12,)),
            pltpu.SemaphoreType.DMA((12,)),
        ],
        compiler_params=pltpu.CompilerParams(
            collective_id=0, has_side_effects=True, vmem_limit_bytes=56 * 1024 * 1024
        ),
        cost_estimate=pl.CostEstimate(
            flops=6_000_000_000, bytes_accessed=12_000_000, transcendentals=3_000_000
        ),
    )(
        grid, *weights, *perms,
        gain_attn.reshape(1, -1), gain_mlp.reshape(1, -1), gain_merge.reshape(1, -1),
        lat_valid, region_ids,
    )
    return merged.transpose(2, 0, 1, 3)


def solution(mesh):
    placed = (P(None, "lat", "lon", None),) + (P(),) * 11
    return jax.shard_map(
        functools.partial(on_device, mesh.shape["lat"], mesh.shape["lon"]),
        mesh=mesh,
        in_specs=placed,
        out_specs=P(None, "lat", "lon", None),
        check_vma=False,
    )
```
